256 devices in a mesh: enc: 4 (over z_lo), seq: 64 (over x, z_hi, y, core).
Axes of the slice: x: 4, y: 4, z: 8 (z_hi: 2, z_lo: 4; z = z_hi * 4 + z_lo), core: 2. Of those that a mesh axis runs over, the one named last changes fastest.
Arguments:
- q_proj: bfloat16 [64, 512, 3072], P('seq', 'enc')
- k_proj: bfloat16 [64, 512, 3072], P('seq', 'enc')
- v_proj: bfloat16 [64, 512, 3072], P('seq', 'enc'), may hold values from -6 to 6
- residual_in: bfloat16 [64, 512, 3072], P('seq', 'enc'), may hold values from -6 to 6
- upstream: bfloat16 [64, 512, 3072], P('seq', 'enc'), may hold values from -3 to 3
- enc_hidden: bfloat16 [64, 512, 1536], P('seq', 'enc')
- enc_gain: float32 [1536], replicated, may hold values from 0.5 to 1.5
- enc_bias: float32 [1536], replicated, may hold values from -3 to 3
- proj_weight: bfloat16 [3072, 1536], P(('enc', 'seq')), may hold values from -0.109375 to 0.109375
- patch_map: int32 [64, 512], P('seq', 'enc'), may hold values from 0 to 511, each once within a row
Outputs:
- d_query: bfloat16 [64, 512, 3072], P('seq', 'enc')
- d_key: bfloat16 [64, 512, 3072], P('seq', 'enc')
- d_value: bfloat16 [64, 512, 3072], P('seq', 'enc')
- d_residual: bfloat16 [64, 512, 3072], P('seq', 'enc')
- w_grad: float32 [3072, 1536], P(('enc', 'seq'))
The draws below stay inside these ranges and needn't reach their ends.
Inputs may be any that keep to these rules, and one draw needn't show every extreme that they name: `patch_map`: each frame's row names every one of the frame's 512 encoder patches exactly once.
All inputs are finite; a program needn't handle non-finite values.
Results may differ from the reference program's by a relative error of at most 0.034.
Values may be sent and summed in bfloat16 or wider, within the bound.
A program may use at most 128 MiB of HBM per device.

```python
import math
import jax
import jax.numpy as jnp
from jax import lax

D = 3072
HEADS = 24
HEAD_DIM = 128
E = 1536
FT = 512
FRAMES = 64


def shared_keys(key):
    return jax.random.normal(jax.random.fold_in(key, 17), (FRAMES, FT, D), jnp.float32)


def draw_k_proj(key, part):
    base_keys = shared_keys(key)
    return base_keys.astype(jnp.bfloat16)


def draw_q_proj(key, part):
    key = jax.random.fold_in(key, 3)
    fresh = jax.random.normal(key, (FRAMES, FT, D), jnp.float32)
    return fresh.astype(jnp.bfloat16)


def draw_enc_hidden(key, part):
    key = jax.random.fold_in(key, 5)
    split_keys = jax.random.split(key, 3)
    noise = jax.random.normal(split_keys[0], (FRAMES, FT, E), jnp.float32)
    row_scale = jnp.exp(jax.random.uniform(split_keys[1], (FRAMES, FT, 1), jnp.float32) * math.log(10.0))
    col_scale = jnp.exp(jax.random.uniform(split_keys[2], (1, 1, E), jnp.float32) * math.log(10.0))
    return (noise * row_scale * col_scale).astype(jnp.bfloat16)


def level_of(stream_key, shape, cuts, smallest, largest):
    gain, own = 1.0, jax.random.fold_in(stream_key, 6)
    for dim, shards_of in cuts:
        heights = jnp.exp(jax.random.uniform(jax.random.fold_in(own, dim), (shards_of,), jnp.float32, smallest / len(cuts), largest / len(cuts)))
        gain = gain * jnp.repeat(heights, shape[dim] // shards_of).reshape([-1 if axis == dim else 1 for axis in range(len(shape))])
    return gain


def gaussian(own_key, shape, spread, most, shards=(), dtype=jnp.bfloat16):
    level = level_of(own_key, shape, shards, -0.22, 0.18) if shards else 1.0
    array = jax.random.normal(own_key, shape, jnp.float32) * spread * level
    return jnp.minimum(jnp.maximum(array, -most), most).astype(dtype)


def setup_inputs(seed: int = 0) -> dict:
    key_of = jax.random.split(jax.random.key(seed), 11)
    return {
        "q_proj": draw_q_proj(jax.random.fold_in(key_of[10], 71), 0),
        "k_proj": draw_k_proj(jax.random.fold_in(key_of[10], 71), 0),
        "v_proj": gaussian(key_of[2], (FRAMES, FT, D), 1.0, 6.0, ((0, 64), (1, 4))),
        "residual_in": gaussian(key_of[3], (FRAMES, FT, D), 1.0, 6.0, ((0, 64), (1, 4))),
        "upstream": gaussian(key_of[4], (FRAMES, FT, D), 0.5, 3.0, ((0, 64), (1, 4))),
        "enc_hidden": draw_enc_hidden(jax.random.fold_in(key_of[10], 71), 0),
        "enc_gain": jnp.clip(1.0 + 0.1 * jax.random.normal(key_of[6], (E,), jnp.float32), 0.5, 1.5),
        "enc_bias": gaussian(key_of[7], (E,), 0.5, 3.0, (), jnp.float32),
        "proj_weight": gaussian(key_of[8], (D, E), D ** -0.5, 0.109375, ((0, 256),)),
        "patch_map": jax.vmap(lambda own: jax.random.permutation(own, FT))(jax.random.split(key_of[9], FRAMES)).reshape((FRAMES, FT)).astype(jnp.int32),
    }


align_coef = 128.0
epsilon = 1e-06

def norm_rows(states, gain_vec, bias_vec):
    values_f = states.astype(jnp.float32)
    row_mean = lax.optimization_barrier(jnp.mean(values_f, axis=-1, keepdims=True))
    row_var = lax.optimization_barrier(jnp.mean((values_f - row_mean) ** 2, axis=-1, keepdims=True))
    return ((values_f - row_mean) * lax.rsqrt(row_var + epsilon) * gain_vec + bias_vec).astype(jnp.bfloat16)

def frame_probs(queries, keys_in):
    attn_scale = HEAD_DIM ** (-0.5)
    qs = queries.astype(jnp.float32).reshape(FT, HEADS, HEAD_DIM)
    ks = keys_in.astype(jnp.float32).reshape(FT, HEADS, HEAD_DIM)
    scores = jnp.einsum('qhd,khd->hqk', qs, ks) * attn_scale
    row_max = lax.optimization_barrier(jnp.max(scores, axis=-1, keepdims=True))
    expo = jnp.exp(scores - row_max)
    return expo / lax.optimization_barrier(jnp.sum(expo, axis=-1, keepdims=True))

def frame_forward(inputs):
    queries, keys_in, values_in, residual = inputs
    attn_probs = frame_probs(queries, keys_in)
    probs_low = attn_probs.astype(jnp.bfloat16).astype(jnp.float32)
    vs = values_in.astype(jnp.float32).reshape(FT, HEADS, HEAD_DIM)
    attn_out = jnp.einsum('hqk,khd->qhd', probs_low, vs).astype(jnp.bfloat16).reshape(FT, D)
    hidden = (residual.astype(jnp.float32) + attn_out.astype(jnp.float32)).astype(jnp.bfloat16)
    return (attn_out, hidden)

def frame_backward(inputs):
    queries, keys_in, values_in, attn_out, d_out = inputs
    attn_scale = HEAD_DIM ** (-0.5)
    attn_probs = frame_probs(queries, keys_in)
    probs_low = attn_probs.astype(jnp.bfloat16).astype(jnp.float32)
    qs = queries.astype(jnp.float32).reshape(FT, HEADS, HEAD_DIM)
    ks = keys_in.astype(jnp.float32).reshape(FT, HEADS, HEAD_DIM)
    vs = values_in.astype(jnp.float32).reshape(FT, HEADS, HEAD_DIM)
    grad_out = d_out.astype(jnp.float32).reshape(FT, HEADS, HEAD_DIM)
    d_value = jnp.einsum('hqk,qhd->khd', probs_low, grad_out).astype(jnp.bfloat16)
    d_probs = jnp.einsum('qhd,khd->hqk', grad_out, vs)
    row_dot = lax.optimization_barrier(jnp.sum(grad_out * attn_out.astype(jnp.float32).reshape(FT, HEADS, HEAD_DIM), axis=-1))
    row_dot = jnp.transpose(row_dot)[:, :, None]
    d_scores = (attn_probs * (d_probs - row_dot) * attn_scale).astype(jnp.bfloat16).astype(jnp.float32)
    d_query = jnp.einsum('hqk,khd->qhd', d_scores, ks).astype(jnp.bfloat16)
    d_key = jnp.einsum('hqk,qhd->khd', d_scores, qs).astype(jnp.bfloat16)
    return (d_query.reshape(FT, D), d_key.reshape(FT, D), d_value.reshape(FT, D))

def align_grad(z_proj, targets):
    target_f32 = targets.astype(jnp.float32)
    norm_z = jnp.sqrt(lax.optimization_barrier(jnp.sum(z_proj * z_proj, axis=-1, keepdims=True)) + epsilon)
    norm_y = jnp.sqrt(lax.optimization_barrier(jnp.sum(target_f32 * target_f32, axis=-1, keepdims=True)) + epsilon)
    cosine = lax.optimization_barrier(jnp.sum(z_proj * target_f32, axis=-1, keepdims=True)) / (norm_z * norm_y)
    return (-align_coef * (target_f32 / (norm_z * norm_y) - cosine * z_proj / (norm_z * norm_z))).astype(jnp.bfloat16)

def reference(q_proj, k_proj, v_proj, residual_in, upstream, enc_hidden, enc_gain, enc_bias, proj_weight, patch_map):
    targets_src = norm_rows(enc_hidden, enc_gain, enc_bias)
    targets = jnp.take_along_axis(targets_src, patch_map.astype(jnp.int32)[:, :, None], axis=1)
    attn_out, hidden = lax.map(frame_forward, (q_proj, k_proj, v_proj, residual_in))
    flat_hidden = hidden.reshape(FRAMES * FT, D)
    z_proj = jnp.dot(flat_hidden, proj_weight, preferred_element_type=jnp.float32)
    d_z = align_grad(z_proj, targets.reshape(FRAMES * FT, E))
    d_align = jnp.dot(d_z, jnp.transpose(proj_weight), preferred_element_type=jnp.float32)
    d_residual = (upstream.astype(jnp.float32) + d_align.reshape(FRAMES, FT, D)).astype(jnp.bfloat16)
    w_grad = jnp.dot(jnp.transpose(flat_hidden), d_z, preferred_element_type=jnp.float32)
    d_query, d_key, d_value = lax.map(frame_backward, (q_proj, k_proj, v_proj, attn_out, d_residual))
    return (d_query, d_key, d_value, d_residual, w_grad)
```

```python
import math

import jax
import jax.numpy as jnp
from jax import lax
from jax.experimental import pallas as pl
from jax.experimental.pallas import tpu as pltpu
from jax.sharding import PartitionSpec as P

HD = 128
D = 3072
E = 1536
FT = 512
TOK = 128
HW = 768
PW = 256
QUARTER = 384
NX, NY, NZH, NE = 4, 4, 2, 4
ALIGN = 128.0
EPS = 1e-6
SCALE = HD**-0.5
SCALE2 = SCALE * math.log2(math.e)
BF = jnp.bfloat16
F32 = jnp.float32
NT = (((1,), (1,)), ((), ()))
NN = (((1,), (0,)), ((), ()))


def mm(a, b, dims=NN):
    return lax.dot_general(a, b, dims, preferred_element_type=F32)


SCRATCH = {
    "encv": ((TOK, E), BF),
    "qh": ((FT, HW), BF),
    "kh": ((FT, HW), BF),
    "vh": ((FT, HW), BF),
    "pt": ((6, FT, FT), BF),
    "ob": ((FT, HW), BF),
    "oh": ((2 * TOK, E), BF),
    "rh": ((2 * TOK, E), BF),
    "uh": ((2 * TOK, E), BF),
    "hid": ((2 * TOK, E), BF),
    "hidt": ((E, 2 * TOK), BF),
    "za": ((2 * TOK, E), F32),
    "zr": ((TOK, E), F32),
    "ts": ((TOK, E), BF),
    "tsl": ((FT, QUARTER), BF),
    "tpm": ((FT, QUARTER), BF),
    "tg": ((TOK, E), BF),
    "pmb": ((NE, 8, 128), jnp.int32),
    "pmo": ((8, 128), jnp.int32),
    "wy": ((2, NZH, NY, 32, E), BF),
    "wh": ((E, E), BF),
    "dzb": ((2 * TOK, E), BF),
    "drs": ((2 * TOK, E), BF),
    "doh": ((FT, HW), BF),
    "dqb": ((FT, HW), BF),
    "dkb": ((FT, HW), BF),
    "dvb": ((FT, HW), BF),
    "gb": ((2, NX, 192, E), BF),
    "gt": ((2, 192, E), BF),
    "gl": ((4, 192, E), BF),
    "gy": ((2, NZH, NY, 32, E), BF),
    "yt": ((2, NZH, 32, E), BF),
    "yl": ((4, NZH, 32, E), BF),
    "gz": ((8, 16, E), BF),
}
NSEM = 400


def kernel(
    q, k, v, res, ups, enc, gain, bias, wpad, pm, dq, dk, dv, dres, wg, *scratch
):
    r = dict(zip(SCRATCH, scratch[: len(SCRATCH)], strict=True))
    sem = scratch[len(SCRATCH)]
    top = [0]

    def sems(n):
        base = top[0]
        top[0] += n
        assert top[0] <= NSEM
        return base

    e = lax.axis_index("enc")
    s = lax.axis_index("seq")
    c = lax.rem(s, 2)
    y = lax.rem(s // 2, NY)
    zh = lax.rem(s // 8, NZH)
    x = s // 16
    o = 1 - c

    def seq_of(xx, zz, yy, cc):
        return ((xx * NZH + zz) * NY + yy) * 2 + cc

    def dev(ee=None, xx=None, zz=None, yy=None, cc=None):
        return (
            e if ee is None else ee,
            seq_of(
                x if xx is None else xx,
                zh if zz is None else zz,
                y if yy is None else yy,
                c if cc is None else cc,
            ),
        )

    sibling = dev(cc=o)
    pending = []

    def put(src, dst, rs, target, here=None):
        ss = sems(1)
        copy = pltpu.make_async_remote_copy(
            src_ref=src,
            dst_ref=dst,
            send_sem=sem.at[ss],
            recv_sem=sem.at[rs],
            device_id=target,
            device_id_type=pl.DeviceIdType.MESH,
        )
        if here is None:
            copy.start()
            pending.append((None, copy))
            return
        away = jnp.logical_not(here)

        @pl.when(here)
        def _():
            pltpu.make_async_copy(src, dst, sem.at[rs]).start()

        @pl.when(away)
        def _():
            copy.start()

        pending.append((away, copy))

    def local(src, dst, rs):
        pltpu.make_async_copy(src, dst, sem.at[rs]).start()

    def wait(dst, rs):
        pltpu.make_async_copy(dst, dst, sem.at[rs]).wait()

    def col(start, width):
        return pl.ds(pl.multiple_of(start, 128), width)

    def row(start, width):
        return pl.ds(pl.multiple_of(start, 16), width)

    barrier = pltpu.get_barrier_semaphore()
    mine = (zh * NE + e) * 2 + c
    greeted = []
    for n in range(1, 16):
        other = lax.rem(mine + n, 16)
        greeted.append(
            dev(ee=lax.rem(other // 2, NE), zz=other // 8, cc=lax.rem(other, 2))
        )
    for step in (1, 3):
        greeted.append(dev(yy=lax.rem(y + step, NY)))
        greeted.append(dev(xx=lax.rem(x + step, NX)))

    enc_sem = sems(1)
    local(enc.at[0], r["encv"], enc_sem)
    qkv_sem = sems(3 * 3 * NE)
    qkv = ((q, r["qh"]), (k, r["kh"]), (v, r["vh"]))
    for p in range(3):
        for a, (src, dst) in enumerate(qkv):
            local(
                src.at[0, :, col(e * HW + p * PW, PW)],
                dst.at[row(e * TOK, TOK), pl.ds(p * PW, PW)],
                qkv_sem + (p * 3 + a) * NE + e,
            )
    half_sem = sems(4)
    local(res.at[0, :, col(c * E, E)], r["rh"].at[row(c * TOK, TOK)], half_sem)
    local(ups.at[0, :, col(c * E, E)], r["uh"].at[row(c * TOK, TOK)], half_sem + 1)

    for target in greeted:
        pl.semaphore_signal(
            barrier, inc=1, device_id=target, device_id_type=pl.DeviceIdType.MESH
        )
    pl.semaphore_wait(barrier, len(greeted))

    half = e // 2
    side = lax.rem(e, 2)
    w_sem = sems(8)
    for n in range(8):
        other = lax.rem(zh * NE + e + n, 8)
        put(
            wpad,
            r["wy"].at[side, zh, y, row(c * 16, 16)],
            w_sem + (side * NZH + zh) * 2 + c,
            dev(ee=lax.rem(other, NE), zz=other // NE, cc=half),
            (half == c) if n == 0 else None,
        )

    def send_qkv(p):
        for n in range(1, NE):
            j = lax.rem(e + n, NE)
            for a, (src, dst) in enumerate(qkv):
                put(
                    src.at[0, :, col(j * HW + p * PW, PW)],
                    dst.at[row(e * TOK, TOK), pl.ds(p * PW, PW)],
                    qkv_sem + (p * 3 + a) * NE + e,
                    dev(ee=j),
                )

    def wait_qkv(p):
        for a, (_, dst) in enumerate(qkv):
            for j in range(NE):
                wait(
                    dst.at[pl.ds(j * TOK, TOK), pl.ds(p * PW, PW)],
                    qkv_sem + (p * 3 + a) * NE + j,
                )

    send_qkv(0)
    put(
        res.at[0, :, col(o * E, E)],
        r["rh"].at[row(c * TOK, TOK)],
        half_sem + 2,
        sibling,
    )
    put(
        ups.at[0, :, col(o * E, E)],
        r["uh"].at[row(c * TOK, TOK)],
        half_sem + 3,
        sibling,
    )

    wait(r["encv"], enc_sem)
    r["pmo"][...] = jnp.broadcast_to(pm[...], (8, 128))

    def norm(i, _):
        rows = row(i * 32, 32)
        t = r["encv"][rows, :].astype(F32)
        mean = jnp.mean(t, axis=-1, keepdims=True)
        t = t - mean
        var = jnp.mean(t * t, axis=-1, keepdims=True)
        r["ts"][rows, :] = (t * lax.rsqrt(var + EPS) * gain[...] + bias[...]).astype(BF)
        return 0

    lax.fori_loop(0, TOK // 32, norm, 0)
    t_sem, pm_sem = sems(NE), sems(NE)
    for n in range(NE):
        j = lax.rem(e + n, NE)
        src = r["ts"].at[:, col(j * QUARTER, QUARTER)]
        dst = r["tsl"].at[row(e * TOK, TOK)]
        if n:
            put(src, dst, t_sem + e, dev(ee=j))
            put(r["pmo"], r["pmb"].at[e], pm_sem + e, dev(ee=j))
        else:
            local(src, dst, t_sem + e)
            local(r["pmo"], r["pmb"].at[e], pm_sem + e)
    send_qkv(1)
    send_qkv(2)

    class Gather:
        def __init__(self, m, to, piece):
            self.m, self.to, self.piece = m, to, piece
            self.sem = sems(6)
            self.up, self.down = lax.rem(m + 1, 4), lax.rem(m + 3, 4)

        def start(self):
            for i in range(2):
                own = self.piece(self.m, i)
                put(own, own, self.sem + i, self.to(self.up))
                put(own, own, self.sem + 2 + i, self.to(self.down))

        def forward(self):
            first = self.piece(self.down, 0)
            wait(first, self.sem)
            put(first, first, self.sem + 4, self.to(self.up))
            second = self.piece(self.up, 1)
            wait(second, self.sem + 3)
            put(second, second, self.sem + 5, self.to(self.down))

        def finish(self):
            wait(self.piece(self.down, 1), self.sem + 1)
            wait(self.piece(self.up, 0), self.sem + 2)
            far = lax.rem(self.m + 2, 4)
            wait(self.piece(far, 0), self.sem + 4)
            wait(self.piece(far, 1), self.sem + 5)

    for i in range(2):
        for zz in range(NZH):
            for cc in range(2):
                wait(
                    r["wy"].at[i, zz, y, pl.ds(cc * 16, 16)],
                    w_sem + (i * NZH + zz) * 2 + cc,
                )
    gather_y = Gather(
        y, lambda m: dev(yy=m), lambda m, i: r["wy"].at[i, :, m]
    )
    gather_y.start()
    gather_y.forward()
    gather_y.finish()
    ri = lax.broadcasted_iota(jnp.int32, (96, 128), 0)
    ci = lax.broadcasted_iota(jnp.int32, (96, 128), 1)
    keep = jnp.logical_and((ci >> 4) * 12 + (ci & 15) == ri, (ci & 15) < 12)
    squeeze = jnp.where(keep, 1.0, 0.0).astype(BF)
    for i in range(2):
        for zz in range(NZH):
            block = r["wy"][i, zz].reshape(128, E)
            r["wh"][row(i * HW + x * 192 + zz * 96, 96), :] = mm(squeeze, block).astype(
                BF
            )
    gather_x = Gather(
        x,
        lambda m: dev(xx=m),
        lambda m, i: r["wh"].at[row(i * HW + m * 192, 192)],
    )
    gather_x.start()

    o_sem = sems(3 * 4)

    def forward(p):
        wait_qkv(p)

        def head(hh, _):
            h = p * 2 + hh
            cols = col(h * HD, HD)
            kk = r["kh"][:, cols]
            vt = jnp.transpose(r["vh"][:, cols])
            for t in range(2):
                rows = pl.ds(t * 256, 256)
                sc = mm(kk, r["qh"][rows, cols], NT)
                ex = jnp.exp2((sc - jnp.max(sc, axis=0, keepdims=True)) * SCALE2)
                pr = (ex * (1.0 / jnp.sum(ex, axis=0, keepdims=True))).astype(BF)
                r["pt"][h, :, rows] = pr
                r["ob"][rows, cols] = jnp.transpose(mm(vt, pr)).astype(BF)
            return 0

        lax.fori_loop(0, 2, head, 0)
        for n in range(NE):
            j = lax.rem(e + n, NE)
            put(
                r["ob"].at[row(j * TOK, TOK), pl.ds(p * PW, PW)],
                r["oh"].at[row(c * TOK, TOK), col(side * HW + p * PW, PW)],
                o_sem + p * 4 + c * 2 + side,
                dev(ee=j, cc=half),
                (half == c) if n == 0 else None,
            )

    forward(0)

    tb_sem = sems(NE)
    for j in range(NE):
        wait(r["tsl"].at[pl.ds(j * TOK, TOK)], t_sem + j)
        wait(r["pmb"].at[j], pm_sem + j)

    def permute(j, _):
        names = r["pmb"][j][0:1, :]
        at = lax.broadcasted_iota(jnp.int32, (FT, TOK), 0)
        pick = jnp.where(at == names, 1.0, 0.0)
        pick = jnp.transpose(pick).astype(BF)
        r["tpm"][row(j * TOK, TOK), :] = mm(pick, r["tsl"][...]).astype(BF)
        return 0

    lax.fori_loop(0, NE, permute, 0)
    for n in range(NE):
        j = lax.rem(e + n, NE)
        src = r["tpm"].at[row(j * TOK, TOK)]
        dst = r["tg"].at[:, col(e * QUARTER, QUARTER)]
        if n:
            put(src, dst, tb_sem + e, dev(ee=j))
        else:
            local(src, dst, tb_sem + e)

    forward(1)
    gather_x.forward()
    forward(2)
    gather_x.finish()

    for n in range(4):
        wait(r["rh" if n % 2 == 0 else "uh"].at[row((c if n < 2 else o) * TOK, TOK)], half_sem + n)

    def hidden(p):
        for i in range(2):
            cols = pl.ds(i * HW + p * PW, PW)
            for f in range(2):
                wait(r["oh"].at[pl.ds(f * TOK, TOK), cols], o_sem + p * 4 + f * 2 + i)
            r["hid"][:, cols] = (
                r["rh"][:, cols].astype(F32) + r["oh"][:, cols].astype(F32)
            ).astype(BF)

    def project(p, rows):
        part = 0.0
        for i in range(2):
            cols = pl.ds(i * HW + p * PW, PW)
            part = part + mm(r["hid"][rows, cols], r["wh"][cols, :])
        return part

    every = pl.ds(0, 2 * TOK)
    hidden(0)
    r["za"][...] = project(0, every)
    hidden(1)
    r["za"][...] += project(1, every)
    hidden(2)
    theirs, ours = row(o * TOK, TOK), row(c * TOK, TOK)
    z_sem = sems(1)
    r["za"][theirs, :] += project(2, theirs)
    put(r["za"].at[theirs], r["zr"], z_sem, sibling)
    r["za"][ours, :] += project(2, ours)
    for j in range(NE):
        wait(r["tg"].at[:, pl.ds(j * QUARTER, QUARTER)], tb_sem + j)
    wait(r["zr"], z_sem)

    def align(i, _):
        rows = row(i * 32, 32)
        z = r["za"][row(c * TOK + i * 32, 32), :] + r["zr"][rows, :]
        t = r["tg"][rows, :].astype(F32)
        nz = jnp.sqrt(jnp.sum(z * z, axis=-1, keepdims=True) + EPS)
        ny = jnp.sqrt(jnp.sum(t * t, axis=-1, keepdims=True) + EPS)
        cosine = jnp.sum(z * t, axis=-1, keepdims=True) / (nz * ny)
        r["dzb"][row(c * TOK + i * 32, 32), :] = (
            -ALIGN * (t * (1.0 / (nz * ny)) - z * (cosine / (nz * nz)))
        ).astype(BF)
        return 0

    lax.fori_loop(0, TOK // 32, align, 0)
    dz_sem = sems(1)
    put(r["dzb"].at[ours], r["dzb"].at[ours], dz_sem, sibling)
    wait(r["dzb"].at[theirs], dz_sem)

    do_sem, dr_sem = sems(3 * NE), sems(2 * 6)
    for p in range(3):
        for i in range(2):
            cols = pl.ds(i * HW + p * PW, PW)
            back = mm(r["dzb"][...], r["wh"][cols, :], NT)
            r["drs"][:, cols] = (r["uh"][:, cols].astype(F32) + back).astype(BF)
            for f in (c, o):
                put(
                    r["drs"].at[row(f * TOK, TOK), cols],
                    r["doh"].at[row(e * TOK, TOK), pl.ds(p * PW, PW)],
                    do_sem + p * NE + e,
                    dev(ee=c * 2 + i, cc=f),
                    (c * 2 + i == e) if f is c else None,
                )
    for p in range(3):
        for i in range(2):
            cols = pl.ds(i * HW + p * PW, PW)
            out = dres.at[0, :, col(c * E + i * HW + p * PW, PW)]
            local(r["drs"].at[ours, cols], out, dr_sem + p * 2 + i)
            put(r["drs"].at[theirs, cols], out, dr_sem + 6 + p * 2 + i, sibling)

    def transpose(i, _):
        cols = col(i * 256, 256)
        r["hidt"][row(i * 256, 256), :] = jnp.transpose(r["hid"][:, cols])
        return 0

    lax.fori_loop(0, 6, transpose, 0)

    def partial(m, i):
        a = r["hidt"][row(i * HW + m * 192, 192), :]

        def tile(n, _):
            cols = col(n * 512, 512)
            r["gb"][i, m, :, cols] = mm(a, r["dzb"][:, cols]).astype(BF)
            return 0

        lax.fori_loop(0, 3, tile, 0)

    class Scatter:
        def __init__(self, m, to, piece, transit, arrive):
            self.m, self.to, self.piece = m, to, piece
            self.transit, self.arrive = transit, arrive
            self.sem = sems(6)
            self.up, self.down = lax.rem(m + 1, 4), lax.rem(m + 3, 4)
            self.far = lax.rem(m + 2, 4)

        def start_far(self):
            put(self.piece(self.far, 0), self.transit(0), self.sem, self.to(self.up))
            put(self.piece(self.far, 1), self.transit(1), self.sem + 1, self.to(self.down))

        def start_near(self):
            put(self.piece(self.up, 1), self.arrive(1), self.sem + 3, self.to(self.up))
            put(self.piece(self.down, 0), self.arrive(2), self.sem + 4, self.to(self.down))

        def add(self, into, *others):
            def step(n, _):
                at = into.at[..., col(n * 512, 512)]
                total = at[...].astype(F32)
                for other in others:
                    total += other[..., col(n * 512, 512)].astype(F32)
                at[...] = total.astype(BF)
                return 0

            lax.fori_loop(0, 3, step, 0)

        def forward(self):
            wait(self.transit(0), self.sem)
            self.add(self.piece(self.up, 0), self.transit(0))
            put(self.piece(self.up, 0), self.arrive(0), self.sem + 2, self.to(self.up))
            wait(self.transit(1), self.sem + 1)
            self.add(self.piece(self.down, 1), self.transit(1))
            put(self.piece(self.down, 1), self.arrive(3), self.sem + 5, self.to(self.down))

        def finish(self):
            for n in range(4):
                wait(self.arrive(n), self.sem + 2 + n)
            self.add(self.piece(self.m, 0), self.arrive(0), self.arrive(2))
            self.add(self.piece(self.m, 1), self.arrive(1), self.arrive(3))

    scatter_x = Scatter(
        x,
        lambda m: dev(xx=m),
        lambda m, i: r["gb"].at[i, m],
        lambda i: r["gt"].at[i],
        lambda n: r["gl"].at[n],
    )
    scatter_y = Scatter(
        y,
        lambda m: dev(yy=m),
        lambda m, i: r["gy"].at[i, :, m],
        lambda i: r["yt"].at[i],
        lambda n: r["yl"].at[n],
    )
    for i in range(2):
        partial(scatter_x.far, i)
    scatter_x.start_far()
    partial(scatter_x.up, 1)
    partial(scatter_x.down, 0)
    scatter_x.start_near()
    partial(scatter_x.up, 0)
    partial(scatter_x.down, 1)
    for i in range(2):
        partial(x, i)

    out_sem = sems(3 * 3 * NE)
    grads = ((r["dqb"], dq), (r["dkb"], dk), (r["dvb"], dv))

    def backward(p):
        for j in range(NE):
            wait(
                r["doh"].at[pl.ds(j * TOK, TOK), pl.ds(p * PW, PW)],
                do_sem + p * NE + j,
            )

        def head(hh, _):
            h = p * 2 + hh
            cols = col(h * HD, HD)
            vv = r["vh"][:, cols]
            kt = jnp.transpose(r["kh"][:, cols])
            gv = gk = 0.0
            for t in range(2):
                rows = pl.ds(t * 256, 256)
                go = r["doh"][rows, cols]
                dp = mm(vv, go, NT)
                low = r["pt"][h, :, rows]
                pr = low.astype(F32)
                dot = jnp.sum(pr * dp, axis=0, keepdims=True)
                ds = (pr * (dp - dot) * SCALE).astype(BF)
                gv = gv + mm(low, go)
                gk = gk + mm(ds, r["qh"][rows, cols])
                r["dqb"][rows, cols] = jnp.transpose(mm(kt, ds)).astype(BF)
            r["dvb"][:, cols] = gv.astype(BF)
            r["dkb"][:, cols] = gk.astype(BF)
            return 0

        lax.fori_loop(0, 2, head, 0)
        for n in range(NE):
            j = lax.rem(e + n, NE)
            for a, (src, dst) in enumerate(grads):
                here = src.at[row(j * TOK, TOK), pl.ds(p * PW, PW)]
                there = dst.at[0, :, col(e * HW + p * PW, PW)]
                rs = out_sem + (p * 3 + a) * NE + e
                if n:
                    put(here, there, rs, dev(ee=j))
                else:
                    local(here, there, rs)

    backward(0)
    backward(1)
    scatter_x.forward()
    backward(2)
    scatter_x.finish()
    rj = lax.broadcasted_iota(jnp.int32, (128, 96), 0)
    cj = lax.broadcasted_iota(jnp.int32, (128, 96), 1)
    keep = jnp.logical_and((rj >> 4) * 12 + (rj & 15) == cj, (rj & 15) < 12)
    spread = jnp.where(keep, 1.0, 0.0).astype(BF)
    for i in range(2):
        for zz in range(NZH):
            block = r["gb"][i, x, pl.ds(zz * 96, 96), :]
            r["gy"][i, zz] = mm(spread, block).astype(BF).reshape(NY, 32, E)
    scatter_y.start_far()
    scatter_y.start_near()
    scatter_y.forward()
    scatter_y.finish()
    gz_sem = sems(8)
    for n in range(8):
        i = lax.rem(side + n // 4, 2)
        zz = lax.rem(zh + (n // 2) % 2, NZH)
        cc = lax.rem(c + n % 2, 2)
        put(
            r["gy"].at[i, zz, y, row(cc * 16, 16)],
            r["gz"].at[zh * NE + e],
            gz_sem + zh * NE + e,
            dev(ee=c * 2 + i, zz=zz, cc=cc),
            (half == c) if n == 0 else None,
        )
    for n in range(8):
        wait(r["gz"].at[n], gz_sem + n)
    total = r["gz"][0].astype(F32)
    for n in range(1, 8):
        total = total + r["gz"][n].astype(F32)
    wg[...] = total

    for p in range(3):
        for i in range(2):
            w = col(o * E + i * HW + p * PW, PW)
            wait(dres.at[0, :, col(c * E + i * HW + p * PW, PW)], dr_sem + p * 2 + i)
            wait(dres.at[0, :, w], dr_sem + 6 + p * 2 + i)
    for p in range(3):
        for a, (_, dst) in enumerate(grads):
            for j in range(NE):
                wait(
                    dst.at[0, :, pl.ds(j * HW + p * PW, PW)],
                    out_sem + (p * 3 + a) * NE + j,
                )
    for away, copy in pending:
        if away is None:
            copy.wait_send()
        else:
            pl.when(away)(copy.wait_send)


def per_device(q, k, v, res, ups, enc, gain, bias, weight, pm):
    wpad = jnp.pad(weight, ((0, 4), (0, 0)))
    hbm = pl.BlockSpec(memory_space=pl.ANY)
    vmem = pl.BlockSpec(memory_space=pltpu.VMEM)
    shape = jax.ShapeDtypeStruct((1, TOK, D), BF)
    outs = pl.pallas_call(
        kernel,
        out_shape=[shape] * 4 + [jax.ShapeDtypeStruct((16, E), F32)],
        in_specs=[hbm] * 6 + [vmem] * 4,
        out_specs=[hbm] * 4 + [vmem],
        scratch_shapes=[pltpu.VMEM(*spec) for spec in SCRATCH.values()]
        + [pltpu.SemaphoreType.DMA((NSEM,))],
        compiler_params=pltpu.CompilerParams(
            collective_id=0, has_side_effects=True, vmem_limit_bytes=56 * 2**20
        ),
        name="align_step",
    )(q, k, v, res, ups, enc, gain.reshape(1, E), bias.reshape(1, E), wpad, pm)
    return (*outs[:4], outs[4][:12])


def solution(mesh):
    token = P("seq", "enc", None)
    rows = P(("enc", "seq"), None)
    return jax.shard_map(
        per_device,
        mesh=mesh,
        in_specs=(token,) * 6 + (P(), P(), rows, P("seq", "enc")),
        out_specs=(token,) * 4 + (rows,),
        check_vma=False,
    )
```

```python
import math

import jax
import jax.numpy as jnp
from jax import lax
from jax.experimental import pallas as pl
from jax.experimental.pallas import tpu as pltpu
from jax.sharding import PartitionSpec as P

HD = 128
D = 3072
E = 1536
FT = 512
TOK = 128
HALF = 64
HW = 768
PW = 256
QUARTER = 384
NX, NY, NZH, NE = 4, 4, 2, 4
ALIGN = 128.0
EPS = 1e-6
SCALE = HD**-0.5
SCALE2 = SCALE * math.log2(math.e)
BF = jnp.bfloat16
F32 = jnp.float32
NT = (((1,), (1,)), ((), ()))
NN = (((1,), (0,)), ((), ()))


def mm(a, b, dims=NN):
    return lax.dot_general(a, b, dims, preferred_element_type=F32)


SCRATCH = {
    "encv": ((TOK, E), BF),
    "qh": ((FT, HW), BF),
    "kh": ((FT, HW), BF),
    "vh": ((FT, HW), BF),
    "pt": ((6, FT, FT), BF),
    "ob": ((FT, HW), BF),
    "oh": ((2 * TOK, E), BF),
    "rh": ((2 * TOK, E), BF),
    "uh": ((2 * TOK, E), BF),
    "hid": ((2 * TOK, E), BF),
    "hidt": ((E, 2 * TOK), BF),
    "hidp": ((NZH, 384, 2 * TOK), BF),
    "za": ((2 * TOK, E), F32),
    "zr": ((TOK, E), F32),
    "ts": ((TOK, E), BF),
    "tsl": ((FT, QUARTER), BF),
    "tpm": ((FT, QUARTER), BF),
    "tg": ((TOK, E), BF),
    "pmb": ((NE, 8, 128), jnp.int32),
    "pmo": ((8, 128), jnp.int32),
    "wp": ((2, NX, NZH, NY, 32, E), BF),
    "wh": ((E, E), BF),
    "wt": ((E, E), BF),
    "dzb": ((2 * TOK, E), BF),
    "drs": ((2 * TOK, E), BF),
    "doh": ((FT, HW), BF),
    "dqb": ((FT, HW), BF),
    "dkb": ((FT, HW), BF),
    "dvb": ((FT, HW), BF),
    "gka": ((FT, HW), F32),
    "gva": ((FT, HW), F32),
    "g0": ((NX, NZH, 96, E), BF),
    "t0": ((NZH, 96, E), BF),
    "l0": ((4, 96, E), BF),
    "gs": ((2, NX, NZH, NY, 32, E), BF),
    "g1": ((NZH, NY, 96, E), BF),
    "t1": ((NZH, 96, E), BF),
    "l1": ((4, 96, E), BF),
    "u0": ((NZH, 32, E), BF),
    "m0": ((4, 32, E), BF),
    "u1": ((NZH, 32, E), BF),
    "m1": ((4, 32, E), BF),
    "gz": ((4, 32, E), BF),
    "gt": ((32, E), BF),
    "gf": ((2, 16, E), BF),
    "wo": ((16, E), BF),
}
NSEM = 133


def kernel(
    q, k, v, res, ups, enc, gain, bias, weight, pm, dq, dk, dv, dres, wg, *scratch
):
    r = dict(zip(SCRATCH, scratch[: len(SCRATCH)], strict=True))
    sem = scratch[len(SCRATCH)]
    top = [0]

    def sems(n):
        base = top[0]
        top[0] += n
        assert top[0] <= NSEM
        return base

    e = lax.axis_index("enc")
    s = lax.axis_index("seq")
    c = lax.rem(s, 2)
    y = lax.rem(s // 2, NY)
    zh = lax.rem(s // 8, NZH)
    x = s // 16
    o = 1 - c
    half = e // 2
    side = lax.rem(e, 2)

    def seq_of(xx, zz, yy, cc):
        return ((xx * NZH + zz) * NY + yy) * 2 + cc

    def dev(ee=None, xx=None, zz=None, yy=None, cc=None):
        return (
            e if ee is None else ee,
            seq_of(
                x if xx is None else xx,
                zh if zz is None else zz,
                y if yy is None else yy,
                c if cc is None else cc,
            ),
        )

    sibling = dev(cc=o)
    line = tuple(lax.rem(e + n, NE) for n in range(NE))
    groups = {}

    class Group:
        def __init__(self, cond):
            self.sem, self.size, self.cond, self.done = sems(1), 0, cond, False

        def add(self, src):
            assert not self.done
            self.size += math.prod(src.shape) * src.dtype.itemsize

    def put(src, dst, rs, target, name, here=None):
        cond = None if here is None else jnp.logical_not(here)
        if name not in groups:
            groups[name] = Group(cond)
        group = groups[name]
        group.add(src)
        copy = pltpu.make_async_remote_copy(
            src_ref=src,
            dst_ref=dst,
            send_sem=sem.at[group.sem],
            recv_sem=sem.at[rs],
            device_id=target,
            device_id_type=pl.DeviceIdType.MESH,
        )
        if here is None:
            copy.start()
            return

        @pl.when(here)
        def _():
            pltpu.make_async_copy(src, dst, sem.at[rs]).start()

        @pl.when(cond)
        def _():
            copy.start()

    def flush(*names):
        for name in names:
            group = groups[name]
            group.done = True
            if group.size % (16 * E * 2):
                assert group.size % (8 * 128 * 4) == 0
                like = r["pmb"].at[pl.ds(0, group.size // (8 * 128 * 4))]
            else:
                like = r["wh"].at[pl.ds(0, group.size // (E * 2))]
            copy = pltpu.make_async_copy(like, like, sem.at[group.sem])
            if group.cond is None:
                copy.wait()
            else:
                pl.when(group.cond)(copy.wait)

    def local(src, dst, rs):
        pltpu.make_async_copy(src, dst, sem.at[rs]).start()

    def wait(dst, rs):
        pltpu.make_async_copy(dst, dst, sem.at[rs]).wait()

    def col(start, width):
        return pl.ds(pl.multiple_of(start, 128), width)

    def row(start, width):
        return pl.ds(pl.multiple_of(start, 16), width)

    barrier = pltpu.get_barrier_semaphore()
    mine = (zh * NE + e) * 2 + c
    greeted = []
    for n in range(1, 16):
        other = lax.rem(mine + n, 16)
        greeted.append(
            dev(ee=lax.rem(other // 2, NE), zz=other // 8, cc=lax.rem(other, 2))
        )
    for step in (1, 3):
        greeted.append(dev(yy=lax.rem(y + step, NY)))
        greeted.append(dev(xx=lax.rem(x + step, NX)))
    for target in greeted:
        pl.semaphore_signal(
            barrier, inc=1, device_id=target, device_id_type=pl.DeviceIdType.MESH
        )

    enc_sem = sems(1)
    local(enc.at[0], r["encv"], enc_sem)
    kv_sem, q_sem = sems(6), sems(6)
    pairs = ((k, r["kh"]), (v, r["vh"]))

    def move_kv(p, a, j, n):
        src, dst = pairs[a]
        src = src.at[0, :, col(j * HW + p * PW, PW)]
        dst = dst.at[row(e * TOK, TOK), pl.ds(p * PW, PW)]
        rs = kv_sem + p * 2 + a
        if n:
            put(src, dst, rs, dev(ee=j), "kv")
        else:
            local(src, dst, rs)

    def move_q(b, p, j, n):
        src = q.at[0, pl.ds(b * HALF, HALF), col(j * HW + p * PW, PW)]
        dst = r["qh"].at[row(b * 256 + e * HALF, HALF), pl.ds(p * PW, PW)]
        rs = q_sem + b * 3 + p
        if n:
            put(src, dst, rs, dev(ee=j), "q")
        else:
            local(src, dst, rs)

    for p in range(3):
        for a in range(2):
            move_kv(p, a, e, 0)
        for b in range(2):
            move_q(b, p, e, 0)
    half_sem = sems(4)
    mine_half = []
    for b in range(2):
        for a, (src, dst) in enumerate(((res, r["rh"]), (ups, r["uh"]))):
            from_rows, to_rows = pl.ds(b * HALF, HALF), row(b * TOK + c * HALF, HALF)
            local(
                src.at[0, from_rows, col(c * E, E)],
                dst.at[to_rows],
                half_sem + b * 2 + a,
            )
            mine_half.append(
                (
                    src.at[0, from_rows, col(o * E, E)],
                    dst.at[to_rows],
                    half_sem + b * 2 + a,
                )
            )

    rj = lax.broadcasted_iota(jnp.int32, (16, 12), 0)
    cj = lax.broadcasted_iota(jnp.int32, (16, 12), 1)
    pad = jnp.where(rj == cj, 1.0, 0.0).astype(BF)
    r["wo"][...] = mm(pad, weight[...]).astype(BF)

    pl.semaphore_wait(barrier, len(greeted))

    far_side = lax.rem(side + half + c, 2)
    w_sem = sems(1)
    shard = r["wp"].at[side, x, zh, y, row(c * 16, 16)]
    put(r["wo"], shard, w_sem, dev(ee=3 - e, cc=half), "w mirror")
    put(r["wo"], shard, w_sem, dev(cc=half), "w own", half == c)
    camp = [
        (lax.rem(zh + n // 2, NZH), lax.rem(half + n // 2, 2), lax.rem(side + n, 2))
        for n in range(4)
    ]

    def send_kv(p):
        for n in range(1, NE):
            for a in range(2):
                move_kv(p, a, line[n], n)

    def send_q(b, p):
        for n in range(1, NE):
            move_q(b, p, line[n], n)

    send_kv(0)
    send_q(0, 0)
    w2_sem = sems(4)
    held = r["wp"].at[far_side, x, zh, y]
    wait(held, w_sem)
    for n, (zz, hh, sd) in enumerate(camp):
        if n:
            put(held, held, w2_sem + zh * 2 + side, dev(ee=hh * 2 + sd, zz=zz), "w")
    for src, dst, rs in mine_half:
        put(src, dst, rs, sibling, "half")

    wait(r["encv"], enc_sem)
    r["pmo"][...] = jnp.broadcast_to(pm[...], (8, 128))

    gain_row, bias_row = gain[...].reshape(1, E), bias[...].reshape(1, E)

    def norm(i, _):
        rows = row(i * 32, 32)
        t = r["encv"][rows, :].astype(F32)
        mean = jnp.mean(t, axis=-1, keepdims=True)
        t = t - mean
        var = jnp.mean(t * t, axis=-1, keepdims=True)
        r["ts"][rows, :] = (t * lax.rsqrt(var + EPS) * gain_row + bias_row).astype(BF)
        return 0

    lax.fori_loop(0, TOK // 32, norm, 0)
    t_sem, pm_sem = sems(1), sems(1)
    for n in (1, 2, 3, 0):
        j = line[n]
        src = r["ts"].at[:, col(j * QUARTER, QUARTER)]
        dst = r["tsl"].at[row(e * TOK, TOK)]
        if n:
            put(src, dst, t_sem, dev(ee=j), "t")
            put(r["pmo"], r["pmb"].at[e], pm_sem, dev(ee=j), "pm")
        else:
            local(src, dst, t_sem)
            local(r["pmo"], r["pmb"].at[e], pm_sem)
    send_kv(1)
    send_q(0, 1)

    class Gather:
        def __init__(self, name, m, to, piece):
            self.name, self.m, self.to, self.piece = name, m, to, piece
            self.sem = sems(6)
            self.up, self.down = lax.rem(m + 1, 4), lax.rem(m + 3, 4)

        def start(self):
            for i in range(2):
                own = self.piece(self.m, i)
                put(own, own, self.sem + i, self.to(self.up), self.name)
                put(own, own, self.sem + 2 + i, self.to(self.down), self.name)

        def forward(self):
            first = self.piece(self.down, 0)
            wait(first, self.sem)
            put(first, first, self.sem + 4, self.to(self.up), self.name)
            second = self.piece(self.up, 1)
            wait(second, self.sem + 3)
            put(second, second, self.sem + 5, self.to(self.down), self.name)

        def finish(self):
            wait(self.piece(self.down, 1), self.sem + 1)
            wait(self.piece(self.up, 0), self.sem + 2)
            far = lax.rem(self.m + 2, 4)
            wait(self.piece(far, 0), self.sem + 4)
            wait(self.piece(far, 1), self.sem + 5)

    def to_x(m):
        return dev(xx=m)

    def to_y(m):
        return dev(yy=m)

    for n, (zz, hh, sd) in enumerate(camp):
        if n:
            i = lax.rem(sd + hh + c, 2)
            wait(r["wp"].at[i, x, zz, y], w2_sem + zz * 2 + sd)
    gather_y0 = Gather("gather y0", y, to_y, lambda m, i: r["wp"].at[0, x, i, m])
    gather_x1 = Gather("gather x1", x, to_x, lambda m, i: r["wp"].at[1, m, i, y])
    gather_x0 = Gather(
        "gather x0", x, to_x, lambda m, i: r["wh"].at[row(m * 192 + i * 96, 96)]
    )
    gather_y1 = Gather("gather y1", y, to_y, lambda m, i: r["wp"].at[1, :, i, m])
    ri = lax.broadcasted_iota(jnp.int32, (96, 128), 0)
    ci = lax.broadcasted_iota(jnp.int32, (96, 128), 1)
    keep = jnp.logical_and((ci >> 4) * 12 + (ci & 15) == ri, (ci & 15) < 12)
    squeeze = jnp.where(keep, 1.0, 0.0).astype(BF)

    def squeeze_block(i, xx, zz):
        block = r["wp"][i, xx, zz].reshape(128, E)
        r["wh"][row(i * HW + xx * 192 + zz * 96, 96), :] = mm(squeeze, block).astype(BF)

    gather_y0.start()
    gather_x1.start()
    gather_y0.forward()
    gather_x1.forward()
    gather_y0.finish()
    for zz in range(NZH):
        squeeze_block(0, x, zz)
    gather_x0.start()
    gather_x1.finish()
    gather_y1.start()

    o_sem = sems(2 * 3 * 2)

    def forward(b, p):
        if b == 0:
            for a, (_, dst) in enumerate(pairs):
                wait(dst.at[:, pl.ds(p * PW, PW)], kv_sem + p * 2 + a)
        wait(r["qh"].at[pl.ds(b * 256, 256), pl.ds(p * PW, PW)], q_sem + b * 3 + p)

        def head(hh, _):
            h = p * 2 + hh
            cols = col(h * HD, HD)
            rows = pl.ds(b * 256, 256)
            sc = mm(r["kh"][:, cols], r["qh"][rows, cols], NT)
            ex = jnp.exp2((sc - jnp.max(sc, axis=0, keepdims=True)) * SCALE2)
            pr = (ex * (1.0 / jnp.sum(ex, axis=0, keepdims=True))).astype(BF)
            r["pt"][h, :, rows] = pr
            out = mm(jnp.transpose(r["vh"][:, cols]), pr)
            r["ob"][rows, cols] = jnp.transpose(out).astype(BF)
            return 0

        lax.fori_loop(0, 2, head, 0)
        for n in (1, 2, 3, 0):
            j = line[n]
            put(
                r["ob"].at[row(b * 256 + j * HALF, HALF), pl.ds(p * PW, PW)],
                r["oh"].at[row(b * TOK + c * HALF, HALF), col(side * HW + p * PW, PW)],
                o_sem + (b * 3 + p) * 2 + side,
                dev(ee=j, cc=half),
                "o" if n else "o own",
                None if n else half == c,
            )

    def hidden(b, p):
        rows = pl.ds(b * TOK, TOK)
        part = 0.0
        for i in range(2):
            cols = pl.ds(i * HW + p * PW, PW)
            wait(r["oh"].at[rows, cols], o_sem + (b * 3 + p) * 2 + i)
            hid = (r["rh"][rows, cols].astype(F32) + r["oh"][rows, cols].astype(F32)).astype(
                BF
            )
            r["hid"][rows, cols] = hid
            part = part + mm(hid, r["wh"][cols, :])
        if p == 0:
            r["za"][rows, :] = part
        else:
            r["za"][rows, :] += part

    z_sem = sems(2)
    dz_sem = sems(2)

    def ours(b):
        return row(b * TOK + c * HALF, HALF)

    def theirs(b):
        return row(b * TOK + o * HALF, HALF)

    def z_sum(b):
        if b == 0:
            for bb in range(2):
                for a, dst in enumerate((r["rh"], r["uh"])):
                    wait(dst.at[pl.ds(bb * TOK, TOK)], half_sem + bb * 2 + a)
        for p in range(3):
            hidden(b, p)
        put(
            r["za"].at[theirs(b)],
            r["zr"].at[pl.ds(b * HALF, HALF)],
            z_sem + b,
            sibling,
            "z",
        )

    def align(b):
        if b == 0:
            wait(r["tg"], tb_sem)
        wait(r["zr"].at[pl.ds(b * HALF, HALF)], z_sem + b)

        def rows_of(i, _):
            rows = row(b * HALF + i * 32, 32)
            at = row(b * TOK + c * HALF + i * 32, 32)
            z = r["za"][at, :] + r["zr"][rows, :]
            t = r["tg"][rows, :].astype(F32)
            nz = jnp.sqrt(jnp.sum(z * z, axis=-1, keepdims=True) + EPS)
            ny = jnp.sqrt(jnp.sum(t * t, axis=-1, keepdims=True) + EPS)
            cosine = jnp.sum(z * t, axis=-1, keepdims=True) / (nz * ny)
            r["dzb"][at, :] = (
                -ALIGN * (t * (1.0 / (nz * ny)) - z * (cosine / (nz * nz)))
            ).astype(BF)
            return 0

        lax.fori_loop(0, HALF // 32, rows_of, 0)
        put(r["dzb"].at[ours(b)], r["dzb"].at[ours(b)], dz_sem + b, sibling, "dz")

    do_sem, dr_sem = sems(2 * 3), sems(2)

    def back(b):
        wait(r["dzb"].at[theirs(b)], dz_sem + b)
        rows = pl.ds(b * TOK, TOK)
        dz = r["dzb"][rows, :]
        for p in range(3):
            for i in range(2):
                cols = pl.ds(i * HW + p * PW, PW)
                part = mm(dz, r["wt"][:, cols])
                r["drs"][rows, cols] = (r["uh"][rows, cols].astype(F32) + part).astype(BF)
                for f in (c, o):
                    put(
                        r["drs"].at[row(b * TOK + f * HALF, HALF), cols],
                        r["doh"].at[row(b * 256 + e * HALF, HALF), pl.ds(p * PW, PW)],
                        do_sem + b * 3 + p,
                        dev(ee=c * 2 + i, cc=f),
                        ("do even", "do odd")[i] if f is c else "do",
                        (c * 2 + i == e) if f is c else None,
                    )
        out = dres.at[0, pl.ds(b * HALF, HALF), col(c * E, E)]
        local(r["drs"].at[ours(b)], out, dr_sem + b)
        put(r["drs"].at[theirs(b)], out, dr_sem + b, sibling, "dres")

    dq_sem, dkv_sem = sems(2), sems(2)
    grads = ((r["dkb"], dk), (r["dvb"], dv))

    def backward(b, p):
        wait(r["doh"].at[pl.ds(b * 256, 256), pl.ds(p * PW, PW)], do_sem + b * 3 + p)

        def head(hh, _):
            h = p * 2 + hh
            cols = col(h * HD, HD)
            rows = pl.ds(b * 256, 256)
            go = r["doh"][rows, cols]
            dp = mm(r["vh"][:, cols], go, NT)
            low = r["pt"][h, :, rows]
            pr = low.astype(F32)
            dot = jnp.sum(pr * dp, axis=0, keepdims=True)
            ds = (pr * (dp - dot) * SCALE).astype(BF)
            gv = mm(low, go)
            gk = mm(ds, r["qh"][rows, cols])
            gq = mm(jnp.transpose(r["kh"][:, cols]), ds)
            r["dqb"][rows, cols] = jnp.transpose(gq).astype(BF)
            if b == 0:
                r["gva"][:, cols] = gv
                r["gka"][:, cols] = gk
            else:
                r["dvb"][:, cols] = (r["gva"][:, cols] + gv).astype(BF)
                r["dkb"][:, cols] = (r["gka"][:, cols] + gk).astype(BF)
            return 0

        lax.fori_loop(0, 2, head, 0)
        for n in (1, 2, 3, 0):
            j = line[n]
            here = r["dqb"].at[row(b * 256 + j * HALF, HALF), pl.ds(p * PW, PW)]
            there = dq.at[0, pl.ds(b * HALF, HALF), col(e * HW + p * PW, PW)]
            if n:
                put(here, there, dq_sem + b, dev(ee=j), "dq")
            else:
                local(here, there, dq_sem + b)
            if b == 0:
                continue
            for a, (src, dst) in enumerate(grads):
                here = src.at[row(j * TOK, TOK), pl.ds(p * PW, PW)]
                there = dst.at[0, :, col(e * HW + p * PW, PW)]
                if n:
                    put(here, there, dkv_sem + a, dev(ee=j), "dkv")
                else:
                    local(here, there, dkv_sem + a)

    di = lax.broadcasted_iota(jnp.int32, (384, 384), 0)
    si = lax.broadcasted_iota(jnp.int32, (384, 384), 1)

    def at_least(value, unit):
        return sum((value >= n * unit).astype(jnp.int32) for n in range(1, 4))

    dy = at_least(di, 96)
    dx = at_least(di - dy * 96, 24)
    swap = jnp.where(di + (dx - dy) * 72 == si, 1.0, 0.0).astype(BF)

    def prepare(b):
        rows = pl.ds(b * TOK, TOK)

        def transpose(i, _):
            cols = col(i * 256, 256)
            r["hidt"][row(i * 256, 256), rows] = jnp.transpose(r["hid"][rows, cols])
            return 0

        lax.fori_loop(0, 6, transpose, 0)
        for zz in range(NZH):
            block = jnp.concatenate(
                [
                    r["hidt"][pl.ds(HW + xx * 192 + zz * 96, 96), rows]
                    for xx in range(NX)
                ],
                axis=0,
            )
            r["hidp"][zz, :, rows] = mm(swap, block).astype(BF)

    forward(0, 0)
    send_kv(2)
    send_q(0, 2)

    tb_sem = sems(1)
    wait(r["tsl"], t_sem)
    wait(r["pmb"], pm_sem)

    def permute(j, _):
        names = r["pmb"][j][0:1, :]
        at = lax.broadcasted_iota(jnp.int32, (FT, TOK), 0)
        pick = jnp.where(at == names, 1.0, 0.0)
        pick = jnp.transpose(pick).astype(BF)
        r["tpm"][row(j * TOK, TOK), :] = mm(pick, r["tsl"][...]).astype(BF)
        return 0

    lax.fori_loop(0, NE, permute, 0)
    for n in (1, 2, 3, 0):
        j = line[n]
        src = r["tpm"].at[row(j * TOK, TOK)]
        dst = r["tg"].at[:, col(e * QUARTER, QUARTER)]
        if n:
            put(src, dst, tb_sem, dev(ee=j), "tb")
        else:
            local(src, dst, tb_sem)

    gather_x0.forward()
    gather_y1.forward()
    forward(0, 1)
    for p in range(3):
        send_q(1, p)
    gather_x0.finish()
    gather_y1.finish()

    def squeeze_side(n, _):
        squeeze_block(1, n // NZH, lax.rem(n, NZH))
        return 0

    lax.fori_loop(0, NX * NZH, squeeze_side, 0)

    def turn(i, _):
        rows = col(i * 256, 256)
        r["wt"][:, rows] = jnp.transpose(r["wh"][rows, :])
        return 0

    lax.fori_loop(0, 6, turn, 0)
    forward(0, 2)
    forward(1, 0)
    z_sum(0)
    forward(1, 1)
    align(0)
    forward(1, 2)
    back(0)
    prepare(0)
    backward(0, 0)
    z_sum(1)
    prepare(1)
    backward(0, 1)
    align(1)
    backward(0, 2)
    back(1)
    early = [name for name in groups if name not in ("dq",)]

    rj = lax.broadcasted_iota(jnp.int32, (128, 96), 0)
    cj = lax.broadcasted_iota(jnp.int32, (128, 96), 1)
    keep = jnp.logical_and((rj >> 4) * 12 + (rj & 15) == cj, (rj & 15) < 12)
    spread = jnp.where(keep, 1.0, 0.0).astype(BF)

    class Scatter:
        def __init__(self, name, m, to, piece, transit, arrive):
            self.name, self.m, self.to, self.piece = name, m, to, piece
            self.transit, self.arrive = transit, arrive
            self.sem = sems(6)
            self.up, self.down = lax.rem(m + 1, 4), lax.rem(m + 3, 4)
            self.far = lax.rem(m + 2, 4)

        def start_far(self):
            put(self.piece(self.far, 0), self.transit(0), self.sem, self.to(self.up), self.name)
            put(self.piece(self.far, 1), self.transit(1), self.sem + 1, self.to(self.down), self.name)

        def start_near(self):
            put(self.piece(self.up, 1), self.arrive(1), self.sem + 3, self.to(self.up), self.name)
            put(self.piece(self.down, 0), self.arrive(2), self.sem + 4, self.to(self.down), self.name)

        def add(self, into, *others):
            def step(n, _):
                at = into.at[..., col(n * 512, 512)]
                total = at[...].astype(F32)
                for other in others:
                    total += other[..., col(n * 512, 512)].astype(F32)
                at[...] = total.astype(BF)
                return 0

            lax.fori_loop(0, 3, step, 0)

        def forward(self):
            wait(self.transit(0), self.sem)
            self.add(self.piece(self.up, 0), self.transit(0))
            put(self.piece(self.up, 0), self.arrive(0), self.sem + 2, self.to(self.up), self.name)
            wait(self.transit(1), self.sem + 1)
            self.add(self.piece(self.down, 1), self.transit(1))
            put(self.piece(self.down, 1), self.arrive(3), self.sem + 5, self.to(self.down), self.name)

        def finish(self):
            for n in range(4):
                wait(self.arrive(n), self.sem + 2 + n)
            self.add(self.piece(self.m, 0), self.arrive(0), self.arrive(2))
            self.add(self.piece(self.m, 1), self.arrive(1), self.arrive(3))

    def scatter(name, m, to, piece, transit, arrive):
        return Scatter(
            name, m, to, piece, lambda i: r[transit].at[i], lambda n: r[arrive].at[n]
        )

    scatter_x0 = scatter("scatter x0", x, to_x, lambda m, i: r["g0"].at[m, i], "t0", "l0")
    scatter_y1 = scatter("scatter y1", y, to_y, lambda m, i: r["g1"].at[i, m], "t1", "l1")
    scatter_y0 = scatter("scatter y0", y, to_y, lambda m, i: r["gs"].at[0, x, i, m], "u0", "m0")
    scatter_x1 = scatter("scatter x1", x, to_x, lambda m, i: r["gs"].at[1, m, i, y], "u1", "m1")

    def partial1(n, _):
        m, zz = n // NZH, lax.rem(n, NZH)
        part = mm(r["hidp"][zz, row(m * 96, 96), :], r["dzb"][...])
        r["g1"][zz, m] = part.astype(BF)
        return 0

    def partial0(m):
        a = r["hidt"][row(m * 192, 192), :]
        part = mm(a, r["dzb"][...]).astype(BF)
        r["g0"][m] = part.reshape(NZH, 96, E)

    partial0(scatter_x0.far)
    scatter_x0.start_far()
    lax.fori_loop(0, NX * NZH, partial1, 0)
    scatter_y1.start_far()
    scatter_y1.start_near()
    partial0(scatter_x0.up)
    partial0(scatter_x0.down)
    scatter_x0.start_near()
    partial0(x)

    backward(1, 0)
    scatter_x0.forward()
    backward(1, 1)
    scatter_y1.forward()
    backward(1, 2)
    flush(*early)
    for b in range(2):
        wait(dres.at[0, pl.ds(b * HALF, HALF)], dr_sem + b)
    scatter_x0.finish()
    for zz in range(NZH):
        part = mm(spread, r["g0"][x, zz]).astype(BF)
        r["gs"][0, x, zz] = part.reshape(NY, 32, E)
    scatter_y0.start_far()
    scatter_y0.start_near()
    scatter_y1.finish()
    for zz in range(NZH):
        part = mm(spread, r["g1"][zz, y]).astype(BF)
        r["gs"][1, :, zz, y] = part.reshape(NX, 32, E)
    scatter_x1.start_far()
    scatter_x1.start_near()
    scatter_y0.forward()
    scatter_x1.forward()
    scatter_y0.finish()
    scatter_x1.finish()
    gz_sem, gf_sem = sems(1), sems(1)
    for n, (zz, hh, sd) in enumerate(camp):
        i = lax.rem(sd + hh + c, 2)
        src, dst = r["gs"].at[i, x, zz, y], r["gz"].at[zh * 2 + side]
        if n:
            put(src, dst, gz_sem, dev(ee=hh * 2 + sd, zz=zz), "gz")
        else:
            local(src, dst, gz_sem)
    flush("scatter x0", "scatter y1", "scatter y0", "scatter x1")
    wait(r["gz"], gz_sem)
    total = r["gz"][0].astype(F32)
    for n in range(1, 4):
        total = total + r["gz"][n].astype(F32)
    r["gt"][...] = total.astype(BF)
    home = half == c
    where = jnp.where(home, e, 3 - e)
    slot = jnp.where(home, 0, 1)
    for cc in range(2):
        put(
            r["gt"].at[pl.ds(cc * 16, 16)],
            r["gf"].at[slot],
            gf_sem,
            dev(ee=where, cc=cc),
            ("gf 0", "gf 1")[cc],
            jnp.logical_and(home, c == cc),
        )
    wait(r["gf"], gf_sem)
    wg[...] = r["gf"][0].astype(F32) + r["gf"][1].astype(F32)

    for b in range(2):
        wait(dq.at[0, pl.ds(b * HALF, HALF)], dq_sem + b)
    wait(dk.at[0], dkv_sem)
    wait(dv.at[0], dkv_sem + 1)
    flush(*(name for name, group in groups.items() if not group.done))


def hand_over(*refs):
    ins, outs, held, sem = refs[:5], refs[5:10], refs[10], refs[11]
    loads, stores = [], []
    for n in range(4):
        for i in range(2):
            rows, at = pl.ds(i * HALF, HALF), n * 2 + i
            loads.append(
                pltpu.make_async_copy(ins[n].at[0, rows], held.at[at], sem.at[at])
            )
            stores.append(
                pltpu.make_async_copy(held.at[at], outs[n].at[0, rows], sem.at[8 + at])
            )
    for load in loads:
        load.start()
    outs[4][...] = ins[4][0:12, :]
    for load, store in zip(loads, stores, strict=True):
        load.wait()
        store.start()
    for store in stores:
        store.wait()


def per_device(q, k, v, res, ups, enc, gain, bias, weight, pm):
    hbm = pl.BlockSpec(memory_space=pl.ANY)
    vmem = pl.BlockSpec(memory_space=pltpu.VMEM)
    shape = jax.ShapeDtypeStruct((1, TOK, D), BF)
    outs = pl.pallas_call(
        kernel,
        out_shape=[shape] * 4 + [jax.ShapeDtypeStruct((16, E), F32)],
        in_specs=[hbm] * 6 + [vmem] * 4,
        out_specs=[hbm] * 4 + [vmem],
        scratch_shapes=[pltpu.VMEM(*spec) for spec in SCRATCH.values()]
        + [pltpu.SemaphoreType.DMA((NSEM,))],
        compiler_params=pltpu.CompilerParams(
            collective_id=0, has_side_effects=True, vmem_limit_bytes=56 * 2**20
        ),
        name="align_step",
    )(q, k, v, res, ups, enc, gain, bias, weight, pm)
    return pl.pallas_call(
        hand_over,
        out_shape=[shape] * 4 + [jax.ShapeDtypeStruct((12, E), F32)],
        in_specs=[hbm] * 4 + [vmem],
        out_specs=[hbm] * 4 + [vmem],
        scratch_shapes=[pltpu.VMEM((8, HALF, D), BF), pltpu.SemaphoreType.DMA((16,))],
        compiler_params=pltpu.CompilerParams(vmem_limit_bytes=56 * 2**20),
        name="hand_over",
    )(*outs)


def solution(mesh):
    token = P("seq", "enc", None)
    rows = P(("enc", "seq"), None)
    return jax.shard_map(
        per_device,
        mesh=mesh,
        in_specs=(token,) * 6 + (P(), P(), rows, P("seq", "enc")),
        out_specs=(token,) * 4 + (rows,),
        check_vma=False,
    )
```

```python
import math

import jax
import jax.numpy as jnp
from jax import lax
from jax.experimental import pallas as pl
from jax.experimental.pallas import tpu as pltpu
from jax.sharding import PartitionSpec as P

HD = 128
D = 3072
E = 1536
FT = 512
TOK = 128
HALF = 64
HW = 768
PW = 256
QUARTER = 384
NX, NY, NZH, NE = 4, 4, 2, 4
ALIGN = 128.0
EPS = 1e-6
SCALE = HD**-0.5
SCALE2 = SCALE * math.log2(math.e)
BF = jnp.bfloat16
F32 = jnp.float32
NT = (((1,), (1,)), ((), ()))
NN = (((1,), (0,)), ((), ()))


def mm(a, b, dims=NN):
    return lax.dot_general(a, b, dims, preferred_element_type=F32)


SCRATCH = {
    "encv": ((TOK, E), BF),
    "qh": ((FT, HW), BF),
    "kh": ((FT, HW), BF),
    "vh": ((FT, HW), BF),
    "pt": ((6, FT, FT), BF),
    "ob": ((FT, HW), BF),
    "oh": ((2 * TOK, E), BF),
    "rh": ((2 * TOK, E), BF),
    "uh": ((3 * TOK, E), BF),
    "hid": ((3 * TOK, E), BF),
    "hidt": ((E, 3 * TOK), BF),
    "hidp": ((NZH, 384, 3 * TOK), BF),
    "za": ((2 * TOK, E), F32),
    "zr": ((TOK, E), F32),
    "ts": ((TOK, E), BF),
    "tsl": ((FT, QUARTER), BF),
    "tpm": ((FT, QUARTER), BF),
    "tg": ((TOK, E), BF),
    "pmb": ((NE, 8, 128), jnp.int32),
    "pmo": ((8, 128), jnp.int32),
    "wp": ((2, NX, NZH, NY, 32, E), BF),
    "wh": ((E, E), BF),
    "wt": ((E, E), BF),
    "dzb": ((3 * TOK, E), BF),
    "drs": ((3 * TOK, E), BF),
    "doh": ((FT, HW), BF),
    "dqb": ((FT, HW), BF),
    "dkb": ((FT, HW), BF),
    "dvb": ((FT, HW), BF),
    "rwp": ((TOK, E), F32),
    "rwx": ((HALF, E), F32),
    "rwo": ((HALF, E), BF),
    "rwi": ((TOK, E), BF),
    "g0": ((NX, NZH, 96, E), BF),
    "t0": ((NZH, 96, E), BF),
    "l0": ((4, 96, E), BF),
    "g1": ((NZH, NY, 96, E), BF),
    "t1": ((NZH, 96, E), BF),
    "l1": ((4, 96, E), BF),
    "u0": ((NZH, 32, E), BF),
    "m0": ((4, 32, E), BF),
    "u1": ((NZH, 32, E), BF),
    "m1": ((4, 32, E), BF),
    "gz": ((4, 32, E), BF),
    "gt": ((32, E), BF),
    "gf": ((2, 16, E), BF),
    "wo": ((16, E), BF),
}
NSEM = 144


def kernel(
    q, k, v, res, ups, enc, gain, bias, weight, pm, dq, dk, dv, dres, wg, *scratch
):
    r = dict(zip(SCRATCH, scratch[: len(SCRATCH)], strict=True))
    r["gs"] = r["wp"]
    sem = scratch[len(SCRATCH)]
    top = [0]

    def sems(n):
        base = top[0]
        top[0] += n
        assert top[0] <= NSEM
        return base

    e = lax.axis_index("enc")
    s = lax.axis_index("seq")
    c = lax.rem(s, 2)
    y = lax.rem(s // 2, NY)
    zh = lax.rem(s // 8, NZH)
    x = s // 16
    o = 1 - c
    half = e // 2
    side = lax.rem(e, 2)
    mirror = 3 - e
    mate = half * 2 + 1 - side
    near = half == c
    far = jnp.logical_not(near)
    group = side * 2 + c

    def seq_of(xx, zz, yy, cc):
        return ((xx * NZH + zz) * NY + yy) * 2 + cc

    def dev(ee=None, xx=None, zz=None, yy=None, cc=None):
        return (
            e if ee is None else ee,
            seq_of(
                x if xx is None else xx,
                zh if zz is None else zz,
                y if yy is None else yy,
                c if cc is None else cc,
            ),
        )

    sibling = dev(cc=o)
    groups = {}

    class Group:
        def __init__(self, cond):
            self.sem, self.size, self.cond, self.done = sems(1), 0, cond, False

        def add(self, src):
            assert not self.done
            self.size += math.prod(src.shape) * src.dtype.itemsize

    def put(src, dst, rs, target, name, here=None, only=None):
        cond = only if here is None else jnp.logical_not(here)
        if name not in groups:
            groups[name] = Group(cond)
        group = groups[name]
        group.add(src)
        copy = pltpu.make_async_remote_copy(
            src_ref=src,
            dst_ref=dst,
            send_sem=sem.at[group.sem],
            recv_sem=sem.at[rs],
            device_id=target,
            device_id_type=pl.DeviceIdType.MESH,
        )
        if cond is None:
            copy.start()
            return
        if here is not None:

            @pl.when(here)
            def _():
                pltpu.make_async_copy(src, dst, sem.at[rs]).start()

        @pl.when(cond)
        def _():
            copy.start()

    def flush(*names):
        for name in names:
            group = groups[name]
            group.done = True
            if group.size % (16 * E * 2):
                assert group.size % (8 * 128 * 4) == 0
                like = r["pmb"].at[pl.ds(0, group.size // (8 * 128 * 4))]
            else:
                like = r["wh"].at[pl.ds(0, group.size // (E * 2))]
            copy = pltpu.make_async_copy(like, like, sem.at[group.sem])
            if group.cond is None:
                copy.wait()
            else:
                pl.when(group.cond)(copy.wait)

    def local(src, dst, rs):
        pltpu.make_async_copy(src, dst, sem.at[rs]).start()

    def wait(dst, rs):
        pltpu.make_async_copy(dst, dst, sem.at[rs]).wait()

    def col(start, width):
        return pl.ds(pl.multiple_of(start, 128), width)

    def row(start, width):
        return pl.ds(pl.multiple_of(start, 16), width)

    barrier = pltpu.get_barrier_semaphore()
    mine = (zh * NE + e) * 2 + c
    greeted = []
    for n in range(1, 16):
        other = lax.rem(mine + n, 16)
        greeted.append(
            dev(ee=lax.rem(other // 2, NE), zz=other // 8, cc=lax.rem(other, 2))
        )
    for step in (1, 3):
        greeted.append(dev(yy=lax.rem(y + step, NY)))
        greeted.append(dev(xx=lax.rem(x + step, NX)))
    for target in greeted:
        pl.semaphore_signal(
            barrier, inc=1, device_id=target, device_id_type=pl.DeviceIdType.MESH
        )

    enc_sem = sems(1)
    local(enc.at[0], r["encv"], enc_sem)
    res_sem, ups_sem = sems(1), sems(2)
    res_rows = row(jnp.where(near, 0, TOK), TOK)
    ups_rows = row(jnp.where(near, 0, 2 * TOK), TOK)
    ups_slot = ups_sem + jnp.where(near, 0, 1)
    local(res.at[0, :, col(c * E, E)], r["rh"].at[res_rows], res_sem)
    local(ups.at[0, :, col(c * E, E)], r["uh"].at[ups_rows], ups_slot)

    rj = lax.broadcasted_iota(jnp.int32, (16, 12), 0)
    cj = lax.broadcasted_iota(jnp.int32, (16, 12), 1)
    pad = jnp.where(rj == cj, 1.0, 0.0).astype(BF)
    r["wo"][...] = mm(pad, weight[...]).astype(BF)

    pl.semaphore_wait(barrier, len(greeted))

    far_side = lax.rem(side + half + c, 2)
    w_sem = sems(1)
    shard = r["wp"].at[side, x, zh, y, row(c * 16, 16)]
    put(r["wo"], shard, w_sem, dev(ee=3 - e, cc=half), "w mirror")
    put(r["wo"], shard, w_sem, dev(cc=half), "w own", half == c)
    camp = [
        (lax.rem(zh + n // 2, NZH), lax.rem(half + n // 2, 2), lax.rem(side + n, 2))
        for n in range(4)
    ]

    qkv_sem = sems(9)
    qkv = ((k, r["kh"]), (v, r["vh"]), (q, r["qh"]))
    workers = [(i, i2, dev(ee=c * 2 + i, cc=i2)) for i in range(2) for i2 in range(2)]

    def is_here(i, i2):
        return jnp.logical_and(c * 2 + i == e, c == i2)

    def send_qkv(p, which=(0, 1, 2)):
        for i, i2, target in workers:
            for a in which:
                src, dst = qkv[a]
                put(
                    src.at[0, :, pl.ds((i * 2 + i2) * HW + p * PW, PW)],
                    dst.at[row(e * TOK, TOK), pl.ds(p * PW, PW)],
                    qkv_sem + p * 3 + a,
                    target,
                    f"qkv {i} {i2}",
                    is_here(i, i2),
                )

    send_qkv(0, (0,))
    w2_sem = sems(4)
    held = r["wp"].at[far_side, x, zh, y]
    wait(held, w_sem)
    for n, (zz, hh, sd) in enumerate(camp):
        if n:
            put(held, held, w2_sem + zh * 2 + side, dev(ee=hh * 2 + sd, zz=zz), "w")
    send_qkv(0, (1, 2))
    put(res.at[0, :, col(o * E, E)], r["rh"].at[res_rows], res_sem, sibling, "res")
    put(ups.at[0, :, col(o * E, E)], r["uh"].at[ups_rows], ups_slot, sibling, "ups")

    wait(r["encv"], enc_sem)
    r["pmo"][...] = jnp.broadcast_to(pm[...], (8, 128))
    gain_row, bias_row = gain[...].reshape(1, E), bias[...].reshape(1, E)

    def norm(i, _):
        rows = row(i * 32, 32)
        t = r["encv"][rows, :].astype(F32)
        mean = jnp.mean(t, axis=-1, keepdims=True)
        t = t - mean
        var = jnp.mean(t * t, axis=-1, keepdims=True)
        r["ts"][rows, :] = (t * lax.rsqrt(var + EPS) * gain_row + bias_row).astype(BF)
        return 0

    lax.fori_loop(0, TOK // 32, norm, 0)
    t_sem, pm_sem = sems(1), sems(1)
    for i, i2, target in workers:
        put(
            r["ts"].at[:, pl.ds((i * 2 + i2) * QUARTER, QUARTER)],
            r["tsl"].at[row(e * TOK, TOK)],
            t_sem,
            target,
            f"t {i} {i2}",
            is_here(i, i2),
        )
        put(
            r["pmo"],
            r["pmb"].at[e],
            pm_sem,
            target,
            f"pm {i} {i2}",
            is_here(i, i2),
        )
    send_qkv(1)

    class Gather:
        def __init__(self, name, m, to, piece):
            self.name, self.m, self.to, self.piece = name, m, to, piece
            self.sem = sems(6)
            self.up, self.down = lax.rem(m + 1, 4), lax.rem(m + 3, 4)

        def start(self):
            for i in range(2):
                own = self.piece(self.m, i)
                put(own, own, self.sem + i, self.to(self.up), self.name)
                put(own, own, self.sem + 2 + i, self.to(self.down), self.name)

        def forward(self):
            first = self.piece(self.down, 0)
            wait(first, self.sem)
            put(first, first, self.sem + 4, self.to(self.up), self.name)
            second = self.piece(self.up, 1)
            wait(second, self.sem + 3)
            put(second, second, self.sem + 5, self.to(self.down), self.name)

        def finish(self):
            wait(self.piece(self.down, 1), self.sem + 1)
            wait(self.piece(self.up, 0), self.sem + 2)
            far = lax.rem(self.m + 2, 4)
            wait(self.piece(far, 0), self.sem + 4)
            wait(self.piece(far, 1), self.sem + 5)

    def to_x(m):
        return dev(xx=m)

    def to_y(m):
        return dev(yy=m)

    for n, (zz, hh, sd) in enumerate(camp):
        if n:
            i = lax.rem(sd + hh + c, 2)
            wait(r["wp"].at[i, x, zz, y], w2_sem + zz * 2 + sd)
    gather_y0 = Gather("gather y0", y, to_y, lambda m, i: r["wp"].at[0, x, i, m])
    gather_x1 = Gather("gather x1", x, to_x, lambda m, i: r["wp"].at[1, m, i, y])
    gather_x0 = Gather(
        "gather x0", x, to_x, lambda m, i: r["wh"].at[row(m * 192 + i * 96, 96)]
    )
    gather_y1 = Gather("gather y1", y, to_y, lambda m, i: r["g1"].at[i, m])
    ri = lax.broadcasted_iota(jnp.int32, (96, 128), 0)
    ci = lax.broadcasted_iota(jnp.int32, (96, 128), 1)
    keep = jnp.logical_and((ci >> 4) * 12 + (ci & 15) == ri, (ci & 15) < 12)
    squeeze = jnp.where(keep, 1.0, 0.0).astype(BF)

    def squeeze_block(i, xx, zz):
        block = r["wp"][i, xx, zz].reshape(128, E)
        r["wh"][row(i * HW + xx * 192 + zz * 96, 96), :] = mm(squeeze, block).astype(BF)

    gather_y0.start()
    gather_x1.start()
    gather_y0.forward()
    gather_x1.forward()
    gather_y0.finish()
    for zz in range(NZH):
        squeeze_block(0, x, zz)
    gather_x0.start()
    gather_x1.finish()
    for zz in range(NZH):
        block = r["wp"][1, :, zz, y].reshape(128, E)
        r["g1"][zz, y] = mm(squeeze, block).astype(BF)
    gather_y1.start()

    o_sem = sems(6)

    def forward(p):
        for a, (_, dst) in enumerate(qkv):
            wait(dst.at[:, pl.ds(p * PW, PW)], qkv_sem + p * 3 + a)

        def head(hh, _):
            h = p * 2 + hh
            cols = col(h * HD, HD)
            kk = r["kh"][:, cols]
            vt = jnp.transpose(r["vh"][:, cols])
            for t in range(2):
                rows = pl.ds(t * 256, 256)
                sc = mm(kk, r["qh"][rows, cols], NT)
                ex = jnp.exp2((sc - jnp.max(sc, axis=0, keepdims=True)) * SCALE2)
                pr = (ex * (1.0 / jnp.sum(ex, axis=0, keepdims=True))).astype(BF)
                r["pt"][h, :, rows] = pr
                r["ob"][rows, cols] = jnp.transpose(mm(vt, pr)).astype(BF)
            return 0

        lax.fori_loop(0, 2, head, 0)
        for chip, name, here in ((mate, "o", None), (e, "o own", side == c)):
            for slot, block in enumerate((chip, 3 - chip)):
                put(
                    r["ob"].at[row(block * TOK, TOK), pl.ds(p * PW, PW)],
                    r["oh"].at[pl.ds(slot * TOK, TOK), col(c * HW + p * PW, PW)],
                    o_sem + p * 2 + c,
                    dev(ee=chip, cc=side),
                    name,
                    here,
                )

    rx_sem, rw_sem = sems(1), sems(1)

    def residual_part():
        wait(r["rh"], res_sem)
        r["rwp"][...] = mm(r["rh"][pl.ds(TOK, TOK), :], r["wh"][...])
        put(r["rwp"].at[row(o * HALF, HALF)], r["rwx"], rx_sem, sibling, "rwx")

    def residual_sum():
        wait(r["rwx"], rx_sem)
        r["rwo"][...] = (r["rwp"][row(c * HALF, HALF), :] + r["rwx"][...]).astype(BF)
        put(
            r["rwo"],
            r["rwi"].at[row(c * HALF, HALF)],
            rw_sem,
            dev(ee=mirror, cc=1),
            "rwo",
        )

    both = pl.ds(0, 2 * TOK)
    first, second, third = (pl.ds(n * TOK, TOK) for n in range(3))
    z_sem, dz_sem = sems(1), sems(1)

    def z_sum():
        for p in range(3):
            part = 0.0
            for i in range(2):
                cols = pl.ds(i * HW + p * PW, PW)
                wait(r["oh"].at[:, cols], o_sem + p * 2 + i)
                r["hid"][first, cols] = (
                    r["rh"][first, cols].astype(F32) + r["oh"][first, cols].astype(F32)
                ).astype(BF)
                r["hid"][second, cols] = r["oh"][second, cols]
                part = part + mm(r["hid"][both, cols], r["wh"][cols, :])
            if p == 0:
                r["za"][...] = part
            else:
                r["za"][...] += part
        theirs = row(o * TOK, TOK)
        put(r["za"].at[theirs], r["zr"], z_sem, sibling, "z")
        r["hid"][third, :] = r["rh"][second, :]

    def align():
        wait(r["tg"], tb_sem)

        @pl.when(c == 1)
        def _():
            wait(r["rwi"], rw_sem)
            r["za"][second, :] += r["rwi"][...].astype(F32)

        wait(r["zr"], z_sem)

        def rows_of(i, _):
            rows, at = row(i * 32, 32), row(c * TOK + i * 32, 32)
            z = r["za"][at, :] + r["zr"][rows, :]
            t = r["tg"][rows, :].astype(F32)
            nz = jnp.sqrt(jnp.sum(z * z, axis=-1, keepdims=True) + EPS)
            ny = jnp.sqrt(jnp.sum(t * t, axis=-1, keepdims=True) + EPS)
            cosine = jnp.sum(z * t, axis=-1, keepdims=True) / (nz * ny)
            r["dzb"][at, :] = (
                -ALIGN * (t * (1.0 / (nz * ny)) - z * (cosine / (nz * nz)))
            ).astype(BF)
            return 0

        lax.fori_loop(0, TOK // 32, rows_of, 0)
        ours, theirs = row(c * TOK, TOK), row(o * TOK, TOK)
        put(r["dzb"].at[ours], r["dzb"].at[ours], dz_sem, sibling, "dz")
        wait(r["dzb"].at[theirs], dz_sem)

    home_sem, pass_sem = sems(1), sems(1)

    def send_home():
        put(
            r["dzb"].at[row(TOK + c * HALF, HALF)],
            r["dzb"].at[row(2 * TOK + c * HALF, HALF)],
            home_sem,
            dev(ee=mirror),
            "home",
        )

    def pass_on():
        rows = r["dzb"].at[row(2 * TOK + c * HALF, HALF)]
        wait(rows, home_sem)
        put(rows, rows, pass_sem, sibling, "pass")

    far_sem, do_sem, dr_sem = sems(6), sems(3), sems(1)

    def send_upstream():
        for p in range(3):
            for h in range(2):
                for i in range(2):
                    cols = pl.ds(i * HW + p * PW, PW)
                    put(
                        ups.at[0, :, pl.ds(h * E + i * HW + p * PW, PW)],
                        r["uh"].at[second, cols],
                        far_sem + p * 2 + i,
                        dev(ee=mirror, cc=h),
                        "far ups",
                        only=far,
                    )

    def back(p):
        if p == 0:
            wait(r["uh"].at[first], ups_sem)
        for i in range(2):
            cols = pl.ds(i * HW + p * PW, PW)
            part = mm(r["dzb"][both, :], r["wt"][:, cols])
            wait(r["uh"].at[second, cols], far_sem + p * 2 + i)
            r["drs"][both, cols] = (r["uh"][both, cols].astype(F32) + part).astype(BF)
            for slot, block in enumerate((e, mirror)):
                put(
                    r["drs"].at[pl.ds(slot * TOK, TOK), cols],
                    r["doh"].at[row(block * TOK, TOK), pl.ds(p * PW, PW)],
                    do_sem + p,
                    dev(ee=half * 2 + c, cc=i),
                    f"do {i}",
                    jnp.logical_and(side == c, c == i),
                )
        if p == 2:
            out = dres.at[0, :, col(c * E, E)]
            put(r["drs"].at[first], out, dr_sem, dev(cc=half), "dres 0", near)

    def back_far():
        wait(r["dzb"].at[row(2 * TOK + o * HALF, HALF)], pass_sem)
        wait(r["uh"].at[third], ups_sem + 1)

        def tile(n, _):
            cols = col(n * 512, 512)
            part = mm(r["dzb"][third, :], r["wt"][:, cols])
            r["drs"][third, cols] = (r["uh"][third, cols].astype(F32) + part).astype(BF)
            return 0

        lax.fori_loop(0, 3, tile, 0)
        out = dres.at[0, :, col(c * E, E)]
        put(r["drs"].at[third], out, dr_sem, dev(cc=1 - half), "dres 2", far)

    out_sem = sems(3)
    grads = ((r["dkb"], dk), (r["dvb"], dv), (r["dqb"], dq))

    def backward(p):
        wait(r["doh"].at[:, pl.ds(p * PW, PW)], do_sem + p)

        def head(hh, _):
            h = p * 2 + hh
            cols = col(h * HD, HD)
            vv = r["vh"][:, cols]
            kt = jnp.transpose(r["kh"][:, cols])
            gv = gk = 0.0
            for t in range(2):
                rows = pl.ds(t * 256, 256)
                go = r["doh"][rows, cols]
                dp = mm(vv, go, NT)
                low = r["pt"][h, :, rows]
                pr = low.astype(F32)
                dot = jnp.sum(pr * dp, axis=0, keepdims=True)
                ds = (pr * (dp - dot) * SCALE).astype(BF)
                gv = gv + mm(low, go)
                gk = gk + mm(ds, r["qh"][rows, cols])
                r["dqb"][rows, cols] = jnp.transpose(mm(kt, ds)).astype(BF)
            r["dvb"][:, cols] = gv.astype(BF)
            r["dkb"][:, cols] = gk.astype(BF)
            return 0

        lax.fori_loop(0, 2, head, 0)
        for n in range(NE):
            j = lax.rem(mirror + n, NE)
            for a, (src, dst) in enumerate(grads):
                put(
                    src.at[row(j * TOK, TOK), pl.ds(p * PW, PW)],
                    dst.at[0, :, col(group * HW + p * PW, PW)],
                    out_sem + a,
                    dev(ee=j, cc=half),
                    f"grad {n}",
                    jnp.logical_and(near, j == e),
                )

    di = lax.broadcasted_iota(jnp.int32, (384, 384), 0)
    si = lax.broadcasted_iota(jnp.int32, (384, 384), 1)

    def at_least(value, unit):
        return sum((value >= n * unit).astype(jnp.int32) for n in range(1, 4))

    dy = at_least(di, 96)
    dx = at_least(di - dy * 96, 24)
    swap = jnp.where(di + (dx - dy) * 72 == si, 1.0, 0.0).astype(BF)

    def prepare():
        def transpose(i, _):
            cols = col(i * 256, 256)
            r["hidt"][row(i * 256, 256), :] = jnp.transpose(r["hid"][:, cols])
            return 0

        lax.fori_loop(0, 6, transpose, 0)
        for zz in range(NZH):
            block = jnp.concatenate(
                [
                    r["hidt"][pl.ds(HW + xx * 192 + zz * 96, 96), :]
                    for xx in range(NX)
                ],
                axis=0,
            )
            r["hidp"][zz] = mm(swap, block).astype(BF)

    forward(0)
    send_qkv(2)

    tb_sem = sems(1)
    wait(r["tsl"], t_sem)
    wait(r["pmb"], pm_sem)

    def permute(j, _):
        names = r["pmb"][j][0:1, :]
        at = lax.broadcasted_iota(jnp.int32, (FT, TOK), 0)
        pick = jnp.where(at == names, 1.0, 0.0)
        pick = jnp.transpose(pick).astype(BF)
        r["tpm"][row(j * TOK, TOK), :] = mm(pick, r["tsl"][...]).astype(BF)
        return 0

    lax.fori_loop(0, NE, permute, 0)
    for chip in (mate, e):
        for slot, block in enumerate((chip, 3 - chip)):
            put(
                r["tpm"].at[row(block * TOK, TOK)],
                r["tg"].at[:, col(group * QUARTER, QUARTER)],
                tb_sem,
                dev(ee=chip, cc=slot),
                f"tb {slot}" if chip is e else "tb",
                c == slot if chip is e else None,
            )

    gather_x0.forward()
    gather_y1.forward()
    forward(1)
    gather_x0.finish()
    gather_y1.finish()

    def unswap(n, _):
        cols = col(n * 512, 512)
        for zz in range(NZH):
            block = r["g1"][zz, :, :, cols].reshape(384, 512)
            block = mm(swap, block).astype(BF)
            for xx in range(NX):
                rows = pl.ds(HW + xx * 192 + zz * 96, 96)
                r["wh"][rows, cols] = block[xx * 96 : xx * 96 + 96]
        return 0

    lax.fori_loop(0, 3, unswap, 0)
    residual_part()
    def turn(i, _):
        rows = col(i * 256, 256)
        r["wt"][:, rows] = jnp.transpose(r["wh"][rows, :])
        return 0

    lax.fori_loop(0, 6, turn, 0)
    residual_sum()

    forward(2)
    send_upstream()
    z_sum()
    prepare()
    align()
    send_home()
    back(0)
    back(1)
    backward(0)
    pass_on()
    back(2)
    backward(1)
    back_far()
    flush("gather y1")
    early = [
        name
        for name, sent in groups.items()
        if not sent.done and not name.startswith("grad")
    ]

    rj = lax.broadcasted_iota(jnp.int32, (128, 96), 0)
    cj = lax.broadcasted_iota(jnp.int32, (128, 96), 1)
    keep = jnp.logical_and((rj >> 4) * 12 + (rj & 15) == cj, (rj & 15) < 12)
    spread = jnp.where(keep, 1.0, 0.0).astype(BF)

    class Scatter:
        def __init__(self, name, m, to, piece, transit, arrive):
            self.name, self.m, self.to, self.piece = name, m, to, piece
            self.transit, self.arrive = transit, arrive
            self.sem = sems(6)
            self.up, self.down = lax.rem(m + 1, 4), lax.rem(m + 3, 4)
            self.far = lax.rem(m + 2, 4)

        def start_far(self):
            put(self.piece(self.far, 0), self.transit(0), self.sem, self.to(self.up), self.name)
            put(self.piece(self.far, 1), self.transit(1), self.sem + 1, self.to(self.down), self.name)

        def start_near(self):
            put(self.piece(self.up, 1), self.arrive(1), self.sem + 3, self.to(self.up), self.name)
            put(self.piece(self.down, 0), self.arrive(2), self.sem + 4, self.to(self.down), self.name)

        def add(self, into, *others):
            def step(n, _):
                at = into.at[..., col(n * 512, 512)]
                total = at[...].astype(F32)
                for other in others:
                    total += other[..., col(n * 512, 512)].astype(F32)
                at[...] = total.astype(BF)
                return 0

            lax.fori_loop(0, 3, step, 0)

        def forward(self):
            wait(self.transit(0), self.sem)
            self.add(self.piece(self.up, 0), self.transit(0))
            put(self.piece(self.up, 0), self.arrive(0), self.sem + 2, self.to(self.up), self.name)
            wait(self.transit(1), self.sem + 1)
            self.add(self.piece(self.down, 1), self.transit(1))
            put(self.piece(self.down, 1), self.arrive(3), self.sem + 5, self.to(self.down), self.name)

        def finish(self):
            for n in range(4):
                wait(self.arrive(n), self.sem + 2 + n)
            self.add(self.piece(self.m, 0), self.arrive(0), self.arrive(2))
            self.add(self.piece(self.m, 1), self.arrive(1), self.arrive(3))

    def scatter(name, m, to, piece, transit, arrive):
        return Scatter(
            name, m, to, piece, lambda i: r[transit].at[i], lambda n: r[arrive].at[n]
        )

    scatter_x0 = scatter("scatter x0", x, to_x, lambda m, i: r["g0"].at[m, i], "t0", "l0")
    scatter_y1 = scatter("scatter y1", y, to_y, lambda m, i: r["g1"].at[i, m], "t1", "l1")
    scatter_y0 = scatter("scatter y0", y, to_y, lambda m, i: r["gs"].at[0, x, i, m], "u0", "m0")
    scatter_x1 = scatter("scatter x1", x, to_x, lambda m, i: r["gs"].at[1, m, i, y], "u1", "m1")

    def partial1(n, _):
        m, zz = n // NZH, lax.rem(n, NZH)
        part = mm(r["hidp"][zz, row(m * 96, 96), :], r["dzb"][...])
        r["g1"][zz, m] = part.astype(BF)
        return 0

    def partial0(m):
        a = r["hidt"][row(m * 192, 192), :]
        part = mm(a, r["dzb"][...]).astype(BF)
        r["g0"][m] = part.reshape(NZH, 96, E)

    partial0(scatter_x0.far)
    scatter_x0.start_far()
    lax.fori_loop(0, NX * NZH, partial1, 0)
    scatter_y1.start_far()
    scatter_y1.start_near()
    partial0(scatter_x0.up)
    partial0(scatter_x0.down)
    scatter_x0.start_near()
    partial0(x)
    backward(2)
    flush(*early)
    scatter_x0.forward()
    scatter_y1.forward()
    wait(dres.at[0], dr_sem)
    scatter_x0.finish()
    for zz in range(NZH):
        part = mm(spread, r["g0"][x, zz]).astype(BF)
        r["gs"][0, x, zz] = part.reshape(NY, 32, E)
    scatter_y0.start_far()
    scatter_y0.start_near()
    scatter_y1.finish()
    for zz in range(NZH):
        part = mm(spread, r["g1"][zz, y]).astype(BF)
        r["gs"][1, :, zz, y] = part.reshape(NX, 32, E)
    scatter_x1.start_far()
    scatter_x1.start_near()
    scatter_y0.forward()
    scatter_x1.forward()
    scatter_y0.finish()
    scatter_x1.finish()
    gz_sem, gf_sem = sems(1), sems(1)
    for n, (zz, hh, sd) in enumerate(camp):
        i = lax.rem(sd + hh + c, 2)
        src, dst = r["gs"].at[i, x, zz, y], r["gz"].at[zh * 2 + side]
        if n:
            put(src, dst, gz_sem, dev(ee=hh * 2 + sd, zz=zz), "gz")
        else:
            local(src, dst, gz_sem)
    flush("scatter x0", "scatter y1", "scatter y0", "scatter x1")
    wait(r["gz"], gz_sem)
    total = r["gz"][0].astype(F32)
    for n in range(1, 4):
        total = total + r["gz"][n].astype(F32)
    r["gt"][...] = total.astype(BF)
    home = half == c
    where = jnp.where(home, e, 3 - e)
    slot = jnp.where(home, 0, 1)
    for cc in range(2):
        put(
            r["gt"].at[pl.ds(cc * 16, 16)],
            r["gf"].at[slot],
            gf_sem,
            dev(ee=where, cc=cc),
            ("gf 0", "gf 1")[cc],
            jnp.logical_and(home, c == cc),
        )
    wait(r["gf"], gf_sem)
    wg[...] = r["gf"][0].astype(F32) + r["gf"][1].astype(F32)

    for a, (_, dst) in enumerate(grads):
        wait(dst.at[0], out_sem + a)
    flush(*(name for name, sent in groups.items() if not sent.done))


def hand_over(*refs):
    ins, outs, sem = refs[:5], refs[5:10], refs[10]
    copies = [
        pltpu.make_async_copy(ins[n].at[0], outs[n].at[0], sem.at[n]) for n in range(4)
    ]
    for copy in copies:
        copy.start()
    outs[4][...] = ins[4][0:12, :]
    for copy in copies:
        copy.wait()


def per_device(q, k, v, res, ups, enc, gain, bias, weight, pm):
    hbm = pl.BlockSpec(memory_space=pltpu.HBM)
    anywhere = pl.BlockSpec(memory_space=pl.ANY)
    vmem = pl.BlockSpec(memory_space=pltpu.VMEM)
    shape = jax.ShapeDtypeStruct((1, TOK, D), BF)
    args = [
        pltpu.with_memory_space_constraint(a, pltpu.HBM)
        for a in (q, k, v, res, ups, enc, gain, bias, weight, pm)
    ]
    outs = pl.pallas_call(
        kernel,
        out_shape=[shape] * 4 + [jax.ShapeDtypeStruct((16, E), F32)],
        in_specs=[hbm] * 6 + [vmem] * 4,
        out_specs=[anywhere] * 4 + [vmem],
        scratch_shapes=[pltpu.VMEM(*spec) for spec in SCRATCH.values()]
        + [pltpu.SemaphoreType.DMA((NSEM,))],
        compiler_params=pltpu.CompilerParams(
            collective_id=0, has_side_effects=True, vmem_limit_bytes=50 * 2**20
        ),
        name="align_step",
    )(*args)
    return pl.pallas_call(
        hand_over,
        out_shape=[shape] * 4 + [jax.ShapeDtypeStruct((12, E), F32)],
        in_specs=[anywhere] * 4 + [vmem],
        out_specs=[hbm] * 4 + [vmem],
        scratch_shapes=[pltpu.SemaphoreType.DMA((4,))],
        compiler_params=pltpu.CompilerParams(vmem_limit_bytes=2**20),
        name="hand_over",
    )(*outs)


def solution(mesh):
    token = P("seq", "enc", None)
    rows = P(("enc", "seq"), None)
    return jax.shard_map(
        per_device,
        mesh=mesh,
        in_specs=(token,) * 6 + (P(), P(), rows, P("seq", "enc")),
        out_specs=(token,) * 4 + (rows,),
        check_vma=False,
    )
```

```python
import math

import jax
import jax.numpy as jnp
from jax import lax
from jax.experimental import pallas as pl
from jax.experimental.pallas import tpu as pltpu
from jax.sharding import PartitionSpec as P

HD = 128
D = 3072
E = 1536
FT = 512
TOK = 128
HALF = 64
HW = 768
PW = 256
QUARTER = 384
NX, NY, NZH, NE = 4, 4, 2, 4
ALIGN = 128.0
EPS = 1e-6
SCALE = HD**-0.5
SCALE2 = SCALE * math.log2(math.e)
BF = jnp.bfloat16
F32 = jnp.float32
NT = (((1,), (1,)), ((), ()))
NN = (((1,), (0,)), ((), ()))


def mm(a, b, dims=NN):
    return lax.dot_general(a, b, dims, preferred_element_type=F32)


SCRATCH = {
    "encv": ((TOK, E), BF),
    "gainv": ((E,), F32),
    "biasv": ((E,), F32),
    "pmv": ((1, TOK), jnp.int32),
    "qh": ((FT, HW), BF),
    "kh": ((FT, HW), BF),
    "vh": ((FT, HW), BF),
    "pt": ((6, FT, FT), BF),
    "ob": ((FT, HW), BF),
    "oh": ((2 * TOK, E), BF),
    "rh": ((2 * TOK, E), BF),
    "uh": ((3 * TOK, E), BF),
    "hid": ((3 * TOK, E), BF),
    "hidt": ((E, 3 * TOK), BF),
    "hidp": ((NZH, 384, 3 * TOK), BF),
    "za": ((2 * TOK, E), F32),
    "zr": ((TOK, E), F32),
    "ts": ((TOK, E), BF),
    "tsl": ((FT, QUARTER), BF),
    "tpm": ((FT, QUARTER), BF),
    "tg": ((TOK, E), BF),
    "pmb": ((NE, 8, 128), jnp.int32),
    "pmo": ((8, 128), jnp.int32),
    "wp": ((2, NX, NZH, NY, 32, E), BF),
    "wh": ((E, E), BF),
    "wt": ((E, E), BF),
    "dzb": ((3 * TOK, E), BF),
    "drs": ((3 * TOK, E), BF),
    "doh": ((FT, HW), BF),
    "dqb": ((FT, HW), BF),
    "dkb": ((FT, HW), BF),
    "dvb": ((FT, HW), BF),
    "rwp": ((TOK, E), F32),
    "rwx": ((HALF, E), F32),
    "rwo": ((HALF, E), BF),
    "rwi": ((TOK, E), BF),
    "g0": ((NX, NZH, 96, E), BF),
    "t0": ((NZH, 96, E), BF),
    "l0": ((4, 96, E), BF),
    "g1": ((NZH, NY, 96, E), BF),
    "t1": ((NZH, 96, E), BF),
    "l1": ((4, 96, E), BF),
    "u0": ((NZH, 32, E), BF),
    "m0": ((4, 32, E), BF),
    "u1": ((NZH, 32, E), BF),
    "m1": ((4, 32, E), BF),
    "gz": ((4, 32, E), BF),
    "gt": ((32, E), BF),
    "gf": ((2, 16, E), BF),
    "wo": ((16, E), BF),
}
NSEM = 147


def kernel(
    q, k, v, res, ups, enc, gain, bias, weight, pm, dq, dk, dv, dres, wg, *scratch
):
    r = dict(zip(SCRATCH, scratch[: len(SCRATCH)], strict=True))
    r["gs"] = r["wp"]
    sem = scratch[len(SCRATCH)]
    top = [0]

    def sems(n):
        base = top[0]
        top[0] += n
        assert top[0] <= NSEM
        return base

    e = lax.axis_index("enc")
    s = lax.axis_index("seq")
    c = lax.rem(s, 2)
    y = lax.rem(s // 2, NY)
    zh = lax.rem(s // 8, NZH)
    x = s // 16
    o = 1 - c
    half = e // 2
    side = lax.rem(e, 2)
    mirror = 3 - e
    mate = half * 2 + 1 - side
    near = half == c
    far = jnp.logical_not(near)
    group = side * 2 + c

    def seq_of(xx, zz, yy, cc):
        return ((xx * NZH + zz) * NY + yy) * 2 + cc

    def dev(ee=None, xx=None, zz=None, yy=None, cc=None):
        return (
            e if ee is None else ee,
            seq_of(
                x if xx is None else xx,
                zh if zz is None else zz,
                y if yy is None else yy,
                c if cc is None else cc,
            ),
        )

    sibling = dev(cc=o)
    groups = {}

    class Group:
        def __init__(self, cond):
            self.sem, self.size, self.cond, self.done = sems(1), 0, cond, False

        def add(self, src):
            assert not self.done
            self.size += math.prod(src.shape) * src.dtype.itemsize

    def put(src, dst, rs, target, name, here=None, only=None):
        cond = only if here is None else jnp.logical_not(here)
        if name not in groups:
            groups[name] = Group(cond)
        group = groups[name]
        group.add(src)
        copy = pltpu.make_async_remote_copy(
            src_ref=src,
            dst_ref=dst,
            send_sem=sem.at[group.sem],
            recv_sem=sem.at[rs],
            device_id=target,
            device_id_type=pl.DeviceIdType.MESH,
        )
        if cond is None:
            copy.start()
            return
        if here is not None:

            @pl.when(here)
            def _():
                pltpu.make_async_copy(src, dst, sem.at[rs]).start()

        @pl.when(cond)
        def _():
            copy.start()

    def flush(*names):
        for name in names:
            group = groups[name]
            group.done = True
            if group.size % (16 * E * 2):
                assert group.size % (8 * 128 * 4) == 0
                like = r["pmb"].at[pl.ds(0, group.size // (8 * 128 * 4))]
            else:
                like = r["wh"].at[pl.ds(0, group.size // (E * 2))]
            copy = pltpu.make_async_copy(like, like, sem.at[group.sem])
            if group.cond is None:
                copy.wait()
            else:
                pl.when(group.cond)(copy.wait)

    def local(src, dst, rs):
        pltpu.make_async_copy(src, dst, sem.at[rs]).start()

    def wait(dst, rs):
        pltpu.make_async_copy(dst, dst, sem.at[rs]).wait()

    def col(start, width):
        return pl.ds(pl.multiple_of(start, 128), width)

    def row(start, width):
        return pl.ds(pl.multiple_of(start, 16), width)

    barrier = pltpu.get_barrier_semaphore()
    mine = (zh * NE + e) * 2 + c
    greeted = []
    for n in range(1, 16):
        other = lax.rem(mine + n, 16)
        greeted.append(
            dev(ee=lax.rem(other // 2, NE), zz=other // 8, cc=lax.rem(other, 2))
        )
    for step in (1, 3):
        greeted.append(dev(yy=lax.rem(y + step, NY)))
        greeted.append(dev(xx=lax.rem(x + step, NX)))
    for target in greeted:
        pl.semaphore_signal(
            barrier, inc=1, device_id=target, device_id_type=pl.DeviceIdType.MESH
        )

    enc_sem = sems(1)
    local(enc.at[0], r["encv"], enc_sem)
    small_sem = sems(3)
    small = ((gain, r["gainv"]), (bias, r["biasv"]), (pm, r["pmv"]))
    for n, (src, dst) in enumerate(small):
        local(src, dst, small_sem + n)
    res_sem, ups_sem = sems(1), sems(2)
    res_rows = row(jnp.where(near, 0, TOK), TOK)
    ups_rows = row(jnp.where(near, 0, 2 * TOK), TOK)
    ups_slot = ups_sem + jnp.where(near, 0, 1)
    local(res.at[0, :, col(c * E, E)], r["rh"].at[res_rows], res_sem)
    local(ups.at[0, :, col(c * E, E)], r["uh"].at[ups_rows], ups_slot)

    rj = lax.broadcasted_iota(jnp.int32, (16, 12), 0)
    cj = lax.broadcasted_iota(jnp.int32, (16, 12), 1)
    pad = jnp.where(rj == cj, 1.0, 0.0).astype(BF)
    r["wo"][...] = mm(pad, weight[...]).astype(BF)

    pl.semaphore_wait(barrier, len(greeted))

    far_side = lax.rem(side + half + c, 2)
    w_sem = sems(1)
    shard = r["wp"].at[side, x, zh, y, row(c * 16, 16)]
    put(r["wo"], shard, w_sem, dev(ee=3 - e, cc=half), "w mirror")
    put(r["wo"], shard, w_sem, dev(cc=half), "w own", half == c)
    camp = [
        (lax.rem(zh + n // 2, NZH), lax.rem(half + n // 2, 2), lax.rem(side + n, 2))
        for n in range(4)
    ]

    qkv_sem = sems(9)
    qkv = ((k, r["kh"]), (v, r["vh"]), (q, r["qh"]))
    workers = [(i, i2, dev(ee=c * 2 + i, cc=i2)) for i in range(2) for i2 in range(2)]

    def is_here(i, i2):
        return jnp.logical_and(c * 2 + i == e, c == i2)

    def send_qkv(p, which=(0, 1, 2)):
        for i, i2, target in workers:
            for a in which:
                src, dst = qkv[a]
                put(
                    src.at[0, :, pl.ds((i * 2 + i2) * HW + p * PW, PW)],
                    dst.at[row(e * TOK, TOK), pl.ds(p * PW, PW)],
                    qkv_sem + p * 3 + a,
                    target,
                    f"qkv {i} {i2}",
                    is_here(i, i2),
                )

    send_qkv(0, (0,))
    w2_sem = sems(4)
    held = r["wp"].at[far_side, x, zh, y]
    wait(held, w_sem)
    for n, (zz, hh, sd) in enumerate(camp):
        if n:
            put(held, held, w2_sem + zh * 2 + side, dev(ee=hh * 2 + sd, zz=zz), "w")
    send_qkv(0, (1, 2))
    put(res.at[0, :, col(o * E, E)], r["rh"].at[res_rows], res_sem, sibling, "res")
    put(ups.at[0, :, col(o * E, E)], r["uh"].at[ups_rows], ups_slot, sibling, "ups")

    wait(r["encv"], enc_sem)
    for n, (_, dst) in enumerate(small):
        wait(dst, small_sem + n)
    r["pmo"][...] = jnp.broadcast_to(r["pmv"][...], (8, 128))
    gain_row, bias_row = r["gainv"][...].reshape(1, E), r["biasv"][...].reshape(1, E)

    def norm(i, _):
        rows = row(i * 32, 32)
        t = r["encv"][rows, :].astype(F32)
        mean = jnp.mean(t, axis=-1, keepdims=True)
        t = t - mean
        var = jnp.mean(t * t, axis=-1, keepdims=True)
        r["ts"][rows, :] = (t * lax.rsqrt(var + EPS) * gain_row + bias_row).astype(BF)
        return 0

    lax.fori_loop(0, TOK // 32, norm, 0)
    t_sem, pm_sem = sems(1), sems(1)
    for i, i2, target in workers:
        put(
            r["ts"].at[:, pl.ds((i * 2 + i2) * QUARTER, QUARTER)],
            r["tsl"].at[row(e * TOK, TOK)],
            t_sem,
            target,
            f"t {i} {i2}",
            is_here(i, i2),
        )
        put(
            r["pmo"],
            r["pmb"].at[e],
            pm_sem,
            target,
            f"pm {i} {i2}",
            is_here(i, i2),
        )

    send_qkv(1)

    class Gather:
        def __init__(self, name, m, to, piece):
            self.name, self.m, self.to, self.piece = name, m, to, piece
            self.sem = sems(6)
            self.up, self.down = lax.rem(m + 1, 4), lax.rem(m + 3, 4)

        def start(self):
            for i in range(2):
                own = self.piece(self.m, i)
                put(own, own, self.sem + i, self.to(self.up), self.name)
                put(own, own, self.sem + 2 + i, self.to(self.down), self.name)

        def forward(self):
            first = self.piece(self.down, 0)
            wait(first, self.sem)
            put(first, first, self.sem + 4, self.to(self.up), self.name)
            second = self.piece(self.up, 1)
            wait(second, self.sem + 3)
            put(second, second, self.sem + 5, self.to(self.down), self.name)

        def finish(self):
            wait(self.piece(self.down, 1), self.sem + 1)
            wait(self.piece(self.up, 0), self.sem + 2)
            far = lax.rem(self.m + 2, 4)
            wait(self.piece(far, 0), self.sem + 4)
            wait(self.piece(far, 1), self.sem + 5)

    def to_x(m):
        return dev(xx=m)

    def to_y(m):
        return dev(yy=m)

    for n, (zz, hh, sd) in enumerate(camp):
        if n:
            i = lax.rem(sd + hh + c, 2)
            wait(r["wp"].at[i, x, zz, y], w2_sem + zz * 2 + sd)
    gather_y0 = Gather("gather y0", y, to_y, lambda m, i: r["wp"].at[0, x, i, m])
    gather_x1 = Gather("gather x1", x, to_x, lambda m, i: r["wp"].at[1, m, i, y])
    gather_x0 = Gather(
        "gather x0", x, to_x, lambda m, i: r["wh"].at[row(m * 192 + i * 96, 96)]
    )
    gather_y1 = Gather("gather y1", y, to_y, lambda m, i: r["g1"].at[i, m])
    ri = lax.broadcasted_iota(jnp.int32, (96, 128), 0)
    ci = lax.broadcasted_iota(jnp.int32, (96, 128), 1)
    keep = jnp.logical_and((ci >> 4) * 12 + (ci & 15) == ri, (ci & 15) < 12)
    squeeze = jnp.where(keep, 1.0, 0.0).astype(BF)

    def squeeze_block(i, xx, zz):
        block = r["wp"][i, xx, zz].reshape(128, E)
        r["wh"][row(i * HW + xx * 192 + zz * 96, 96), :] = mm(squeeze, block).astype(BF)

    gather_y0.start()
    gather_x1.start()
    gather_y0.forward()
    gather_x1.forward()
    gather_y0.finish()
    for zz in range(NZH):
        squeeze_block(0, x, zz)
    gather_x0.start()
    gather_x1.finish()
    for zz in range(NZH):
        block = r["wp"][1, :, zz, y].reshape(128, E)
        r["g1"][zz, y] = mm(squeeze, block).astype(BF)
    gather_y1.start()

    o_sem = sems(6)

    def forward(p):
        for a, (_, dst) in enumerate(qkv):
            wait(dst.at[:, pl.ds(p * PW, PW)], qkv_sem + p * 3 + a)

        def head(hh, _):
            h = p * 2 + hh
            cols = col(h * HD, HD)
            kk = r["kh"][:, cols]
            vt = jnp.transpose(r["vh"][:, cols])
            for t in range(2):
                rows = pl.ds(t * 256, 256)
                sc = mm(kk, r["qh"][rows, cols], NT)
                ex = jnp.exp2((sc - jnp.max(sc, axis=0, keepdims=True)) * SCALE2)
                pr = (ex * (1.0 / jnp.sum(ex, axis=0, keepdims=True))).astype(BF)
                r["pt"][h, :, rows] = pr
                r["ob"][rows, cols] = jnp.transpose(mm(vt, pr)).astype(BF)
            return 0

        lax.fori_loop(0, 2, head, 0)
        for chip, name, here in ((mate, "o", None), (e, "o own", side == c)):
            for slot, block in enumerate((chip, 3 - chip)):
                put(
                    r["ob"].at[row(block * TOK, TOK), pl.ds(p * PW, PW)],
                    r["oh"].at[pl.ds(slot * TOK, TOK), col(c * HW + p * PW, PW)],
                    o_sem + p * 2 + c,
                    dev(ee=chip, cc=side),
                    name,
                    here,
                )

    rx_sem, rw_sem = sems(1), sems(1)

    def residual_part():
        wait(r["rh"], res_sem)
        r["rwp"][...] = mm(r["rh"][pl.ds(TOK, TOK), :], r["wh"][...])
        put(r["rwp"].at[row(o * HALF, HALF)], r["rwx"], rx_sem, sibling, "rwx")

    def residual_sum():
        wait(r["rwx"], rx_sem)
        r["rwo"][...] = (r["rwp"][row(c * HALF, HALF), :] + r["rwx"][...]).astype(BF)
        put(
            r["rwo"],
            r["rwi"].at[row(c * HALF, HALF)],
            rw_sem,
            dev(ee=mirror, cc=1),
            "rwo",
        )

    both = pl.ds(0, 2 * TOK)
    first, second, third = (pl.ds(n * TOK, TOK) for n in range(3))
    z_sem, dz_sem = sems(1), sems(1)

    def z_sum():
        for p in range(3):
            part = 0.0
            for i in range(2):
                cols = pl.ds(i * HW + p * PW, PW)
                wait(r["oh"].at[:, cols], o_sem + p * 2 + i)
                r["hid"][first, cols] = (
                    r["rh"][first, cols].astype(F32) + r["oh"][first, cols].astype(F32)
                ).astype(BF)
                r["hid"][second, cols] = r["oh"][second, cols]
                part = part + mm(r["hid"][both, cols], r["wh"][cols, :])
            if p == 0:
                r["za"][...] = part
            else:
                r["za"][...] += part
        theirs = row(o * TOK, TOK)
        put(r["za"].at[theirs], r["zr"], z_sem, sibling, "z")
        r["hid"][third, :] = r["rh"][second, :]

    def align():
        wait(r["tg"], tb_sem)

        @pl.when(c == 1)
        def _():
            wait(r["rwi"], rw_sem)
            r["za"][second, :] += r["rwi"][...].astype(F32)

        wait(r["zr"], z_sem)

        def rows_of(i, _):
            rows, at = row(i * 32, 32), row(c * TOK + i * 32, 32)
            z = r["za"][at, :] + r["zr"][rows, :]
            t = r["tg"][rows, :].astype(F32)
            nz = jnp.sqrt(jnp.sum(z * z, axis=-1, keepdims=True) + EPS)
            ny = jnp.sqrt(jnp.sum(t * t, axis=-1, keepdims=True) + EPS)
            cosine = jnp.sum(z * t, axis=-1, keepdims=True) / (nz * ny)
            r["dzb"][at, :] = (
                -ALIGN * (t * (1.0 / (nz * ny)) - z * (cosine / (nz * nz)))
            ).astype(BF)
            return 0

        lax.fori_loop(0, TOK // 32, rows_of, 0)
        ours, theirs = row(c * TOK, TOK), row(o * TOK, TOK)
        put(r["dzb"].at[ours], r["dzb"].at[ours], dz_sem, sibling, "dz")
        wait(r["dzb"].at[theirs], dz_sem)

    home_sem, pass_sem = sems(1), sems(1)

    def send_home():
        put(
            r["dzb"].at[row(TOK + c * HALF, HALF)],
            r["dzb"].at[row(2 * TOK + c * HALF, HALF)],
            home_sem,
            dev(ee=mirror),
            "home",
        )

    def pass_on():
        rows = r["dzb"].at[row(2 * TOK + c * HALF, HALF)]
        wait(rows, home_sem)
        put(rows, rows, pass_sem, sibling, "pass")

    far_sem, do_sem, dr_sem = sems(6), sems(3), sems(1)

    def send_upstream():
        for p in range(3):
            for h in range(2):
                for i in range(2):
                    cols = pl.ds(i * HW + p * PW, PW)
                    put(
                        ups.at[0, :, pl.ds(h * E + i * HW + p * PW, PW)],
                        r["uh"].at[second, cols],
                        far_sem + p * 2 + i,
                        dev(ee=mirror, cc=h),
                        "far ups",
                        only=far,
                    )

    def back(p):
        if p == 0:
            wait(r["uh"].at[first], ups_sem)
        for i in range(2):
            cols = pl.ds(i * HW + p * PW, PW)
            part = mm(r["dzb"][both, :], r["wt"][:, cols])
            wait(r["uh"].at[second, cols], far_sem + p * 2 + i)
            r["drs"][both, cols] = (r["uh"][both, cols].astype(F32) + part).astype(BF)
            for slot, block in enumerate((e, mirror)):
                put(
                    r["drs"].at[pl.ds(slot * TOK, TOK), cols],
                    r["doh"].at[row(block * TOK, TOK), pl.ds(p * PW, PW)],
                    do_sem + p,
                    dev(ee=half * 2 + c, cc=i),
                    f"do {i}",
                    jnp.logical_and(side == c, c == i),
                )
        if p == 2:
            out = dres.at[0, :, col(c * E, E)]
            put(r["drs"].at[first], out, dr_sem, dev(cc=half), "dres 0", near)

    def back_far():
        wait(r["dzb"].at[row(2 * TOK + o * HALF, HALF)], pass_sem)
        wait(r["uh"].at[third], ups_sem + 1)

        def tile(n, _):
            cols = col(n * 512, 512)
            part = mm(r["dzb"][third, :], r["wt"][:, cols])
            r["drs"][third, cols] = (r["uh"][third, cols].astype(F32) + part).astype(BF)
            return 0

        lax.fori_loop(0, 3, tile, 0)
        out = dres.at[0, :, col(c * E, E)]
        put(r["drs"].at[third], out, dr_sem, dev(cc=1 - half), "dres 2", far)

    out_sem = sems(3)
    grads = ((r["dkb"], dk), (r["dvb"], dv), (r["dqb"], dq))

    def backward(p):
        wait(r["doh"].at[:, pl.ds(p * PW, PW)], do_sem + p)

        def head(hh, _):
            h = p * 2 + hh
            cols = col(h * HD, HD)
            vv = r["vh"][:, cols]
            kt = jnp.transpose(r["kh"][:, cols])
            gv = gk = 0.0
            for t in range(2):
                rows = pl.ds(t * 256, 256)
                go = r["doh"][rows, cols]
                dp = mm(vv, go, NT)
                low = r["pt"][h, :, rows]
                pr = low.astype(F32)
                dot = jnp.sum(pr * dp, axis=0, keepdims=True)
                ds = (pr * (dp - dot) * SCALE).astype(BF)
                gv = gv + mm(low, go)
                gk = gk + mm(ds, r["qh"][rows, cols])
                r["dqb"][rows, cols] = jnp.transpose(mm(kt, ds)).astype(BF)
            r["dvb"][:, cols] = gv.astype(BF)
            r["dkb"][:, cols] = gk.astype(BF)
            return 0

        lax.fori_loop(0, 2, head, 0)
        for n in range(NE):
            j = lax.rem(mirror + n, NE)
            for a, (src, dst) in enumerate(grads):
                put(
                    src.at[row(j * TOK, TOK), pl.ds(p * PW, PW)],
                    dst.at[0, :, col(group * HW + p * PW, PW)],
                    out_sem + a,
                    dev(ee=j, cc=half),
                    f"grad {n}",
                    jnp.logical_and(near, j == e),
                )

    di = lax.broadcasted_iota(jnp.int32, (384, 384), 0)
    si = lax.broadcasted_iota(jnp.int32, (384, 384), 1)

    def at_least(value, unit):
        return sum((value >= n * unit).astype(jnp.int32) for n in range(1, 4))

    dy = at_least(di, 96)
    dx = at_least(di - dy * 96, 24)
    swap = jnp.where(di + (dx - dy) * 72 == si, 1.0, 0.0).astype(BF)

    def prepare():
        def transpose(i, _):
            cols = col(i * 256, 256)
            r["hidt"][row(i * 256, 256), :] = jnp.transpose(r["hid"][:, cols])
            return 0

        lax.fori_loop(0, 6, transpose, 0)
        for zz in range(NZH):
            block = jnp.concatenate(
                [
                    r["hidt"][pl.ds(HW + xx * 192 + zz * 96, 96), :]
                    for xx in range(NX)
                ],
                axis=0,
            )
            r["hidp"][zz] = mm(swap, block).astype(BF)

    forward(0)

    tb_sem = sems(1)
    wait(r["tsl"], t_sem)
    wait(r["pmb"], pm_sem)

    def permute(j, _):
        names = r["pmb"][j][0:1, :]
        at = lax.broadcasted_iota(jnp.int32, (FT, TOK), 0)
        pick = jnp.where(at == names, 1.0, 0.0)
        pick = jnp.transpose(pick).astype(BF)
        r["tpm"][row(j * TOK, TOK), :] = mm(pick, r["tsl"][...]).astype(BF)
        return 0

    lax.fori_loop(0, NE, permute, 0)
    for chip in (mate, e):
        for slot, block in enumerate((chip, 3 - chip)):
            put(
                r["tpm"].at[row(block * TOK, TOK)],
                r["tg"].at[:, col(group * QUARTER, QUARTER)],
                tb_sem,
                dev(ee=chip, cc=slot),
                f"tb {slot}" if chip is e else "tb",
                c == slot if chip is e else None,
            )

    send_qkv(2)
    gather_x0.forward()
    gather_y1.forward()
    forward(1)
    gather_x0.finish()
    gather_y1.finish()

    def unswap(n, _):
        cols = col(n * 512, 512)
        for zz in range(NZH):
            block = r["g1"][zz, :, :, cols].reshape(384, 512)
            block = mm(swap, block).astype(BF)
            for xx in range(NX):
                rows = pl.ds(HW + xx * 192 + zz * 96, 96)
                r["wh"][rows, cols] = block[xx * 96 : xx * 96 + 96]
        return 0

    lax.fori_loop(0, 3, unswap, 0)
    residual_part()
    def turn(i, _):
        rows = col(i * 256, 256)
        r["wt"][:, rows] = jnp.transpose(r["wh"][rows, :])
        return 0

    lax.fori_loop(0, 6, turn, 0)
    residual_sum()

    forward(2)
    send_upstream()
    z_sum()
    align()
    send_home()
    back(0)
    back(1)
    backward(0)
    prepare()
    pass_on()
    back(2)
    backward(1)
    back_far()
    flush("gather y1")
    early = [
        name
        for name, sent in groups.items()
        if not sent.done and not name.startswith("grad")
    ]

    rj = lax.broadcasted_iota(jnp.int32, (128, 96), 0)
    cj = lax.broadcasted_iota(jnp.int32, (128, 96), 1)
    keep = jnp.logical_and((rj >> 4) * 12 + (rj & 15) == cj, (rj & 15) < 12)
    spread = jnp.where(keep, 1.0, 0.0).astype(BF)

    class Scatter:
        def __init__(self, name, m, to, piece, transit, arrive):
            self.name, self.m, self.to, self.piece = name, m, to, piece
            self.transit, self.arrive = transit, arrive
            self.sem = sems(6)
            self.up, self.down = lax.rem(m + 1, 4), lax.rem(m + 3, 4)
            self.far = lax.rem(m + 2, 4)

        def start_far(self):
            put(self.piece(self.far, 0), self.transit(0), self.sem, self.to(self.up), self.name)
            put(self.piece(self.far, 1), self.transit(1), self.sem + 1, self.to(self.down), self.name)

        def start_near(self):
            put(self.piece(self.up, 1), self.arrive(1), self.sem + 3, self.to(self.up), self.name)
            put(self.piece(self.down, 0), self.arrive(2), self.sem + 4, self.to(self.down), self.name)

        def add(self, into, *others):
            def step(n, _):
                at = into.at[..., col(n * 512, 512)]
                total = at[...].astype(F32)
                for other in others:
                    total += other[..., col(n * 512, 512)].astype(F32)
                at[...] = total.astype(BF)
                return 0

            lax.fori_loop(0, 3, step, 0)

        def forward(self):
            wait(self.transit(0), self.sem)
            self.add(self.piece(self.up, 0), self.transit(0))
            put(self.piece(self.up, 0), self.arrive(0), self.sem + 2, self.to(self.up), self.name)
            wait(self.transit(1), self.sem + 1)
            self.add(self.piece(self.down, 1), self.transit(1))
            put(self.piece(self.down, 1), self.arrive(3), self.sem + 5, self.to(self.down), self.name)

        def finish(self):
            for n in range(4):
                wait(self.arrive(n), self.sem + 2 + n)
            self.add(self.piece(self.m, 0), self.arrive(0), self.arrive(2))
            self.add(self.piece(self.m, 1), self.arrive(1), self.arrive(3))

    def scatter(name, m, to, piece, transit, arrive):
        return Scatter(
            name, m, to, piece, lambda i: r[transit].at[i], lambda n: r[arrive].at[n]
        )

    scatter_x0 = scatter("scatter x0", x, to_x, lambda m, i: r["g0"].at[m, i], "t0", "l0")
    scatter_y1 = scatter("scatter y1", y, to_y, lambda m, i: r["g1"].at[i, m], "t1", "l1")
    scatter_y0 = scatter("scatter y0", y, to_y, lambda m, i: r["gs"].at[0, x, i, m], "u0", "m0")
    scatter_x1 = scatter("scatter x1", x, to_x, lambda m, i: r["gs"].at[1, m, i, y], "u1", "m1")

    def partial1(n, _):
        m, zz = n // NZH, lax.rem(n, NZH)
        part = mm(r["hidp"][zz, row(m * 96, 96), :], r["dzb"][...])
        r["g1"][zz, m] = part.astype(BF)
        return 0

    def partial0(m):
        a = r["hidt"][row(m * 192, 192), :]
        part = mm(a, r["dzb"][...]).astype(BF)
        r["g0"][m] = part.reshape(NZH, 96, E)

    partial0(scatter_x0.far)
    scatter_x0.start_far()
    lax.fori_loop(0, NX * NZH, partial1, 0)
    scatter_y1.start_far()
    scatter_y1.start_near()
    partial0(scatter_x0.up)
    partial0(scatter_x0.down)
    scatter_x0.start_near()
    partial0(x)
    backward(2)
    flush(*early)
    scatter_x0.forward()
    scatter_y1.forward()
    wait(dres.at[0], dr_sem)
    scatter_x0.finish()
    for zz in range(NZH):
        part = mm(spread, r["g0"][x, zz]).astype(BF)
        r["gs"][0, x, zz] = part.reshape(NY, 32, E)
    scatter_y0.start_far()
    scatter_y0.start_near()
    scatter_y1.finish()
    for zz in range(NZH):
        part = mm(spread, r["g1"][zz, y]).astype(BF)
        r["gs"][1, :, zz, y] = part.reshape(NX, 32, E)
    scatter_x1.start_far()
    scatter_x1.start_near()
    scatter_y0.forward()
    scatter_x1.forward()
    scatter_y0.finish()
    scatter_x1.finish()
    gz_sem, gf_sem = sems(1), sems(1)
    for n, (zz, hh, sd) in enumerate(camp):
        i = lax.rem(sd + hh + c, 2)
        src, dst = r["gs"].at[i, x, zz, y], r["gz"].at[zh * 2 + side]
        if n:
            put(src, dst, gz_sem, dev(ee=hh * 2 + sd, zz=zz), "gz")
        else:
            local(src, dst, gz_sem)
    flush("scatter x0", "scatter y1", "scatter y0", "scatter x1")
    wait(r["gz"], gz_sem)
    total = r["gz"][0].astype(F32)
    for n in range(1, 4):
        total = total + r["gz"][n].astype(F32)
    r["gt"][...] = total.astype(BF)
    home = half == c
    where = jnp.where(home, e, 3 - e)
    slot = jnp.where(home, 0, 1)
    for cc in range(2):
        put(
            r["gt"].at[pl.ds(cc * 16, 16)],
            r["gf"].at[slot],
            gf_sem,
            dev(ee=where, cc=cc),
            ("gf 0", "gf 1")[cc],
            jnp.logical_and(home, c == cc),
        )
    wait(r["gf"], gf_sem)
    wg[...] = r["gf"][0].astype(F32) + r["gf"][1].astype(F32)

    for a, (_, dst) in enumerate(grads):
        wait(dst.at[0], out_sem + a)
    flush(*(name for name, sent in groups.items() if not sent.done))


def hand_over(*refs):
    ins, outs, sem = refs[:5], refs[5:10], refs[10]
    copies = [
        pltpu.make_async_copy(ins[n].at[0], outs[n].at[0], sem.at[n]) for n in range(4)
    ]
    for copy in copies:
        copy.start()
    outs[4][...] = ins[4][0:12, :]
    for copy in copies:
        copy.wait()


def per_device(q, k, v, res, ups, enc, gain, bias, weight, pm):
    hbm = pl.BlockSpec(memory_space=pltpu.HBM)
    anywhere = pl.BlockSpec(memory_space=pl.ANY)
    vmem = pl.BlockSpec(memory_space=pltpu.VMEM)
    shape = jax.ShapeDtypeStruct((1, TOK, D), BF)
    args = [
        pltpu.with_memory_space_constraint(a, pltpu.HBM)
        for a in (q, k, v, res, ups, enc, gain, bias, weight, pm)
    ]
    outs = pl.pallas_call(
        kernel,
        out_shape=[shape] * 4 + [jax.ShapeDtypeStruct((16, E), F32)],
        in_specs=[hbm] * 8 + [vmem, hbm],
        out_specs=[anywhere] * 4 + [vmem],
        scratch_shapes=[pltpu.VMEM(*spec) for spec in SCRATCH.values()]
        + [pltpu.SemaphoreType.DMA((NSEM,))],
        compiler_params=pltpu.CompilerParams(
            collective_id=0, has_side_effects=True, vmem_limit_bytes=50 * 2**20
        ),
        name="align_step",
    )(*args)
    return pl.pallas_call(
        hand_over,
        out_shape=[shape] * 4 + [jax.ShapeDtypeStruct((12, E), F32)],
        in_specs=[anywhere] * 4 + [vmem],
        out_specs=[hbm] * 4 + [vmem],
        scratch_shapes=[pltpu.SemaphoreType.DMA((4,))],
        compiler_params=pltpu.CompilerParams(vmem_limit_bytes=2**20),
        name="hand_over",
    )(*outs)


def solution(mesh):
    token = P("seq", "enc", None)
    rows = P(("enc", "seq"), None)
    return jax.shard_map(
        per_device,
        mesh=mesh,
        in_specs=(token,) * 6 + (P(), P(), rows, P("seq", "enc")),
        out_specs=(token,) * 4 + (rows,),
        check_vma=False,
    )
```
